256 devices in a mesh: dp: 4 (over z_hi, core), fsdp: 64 (over y, x, z_lo).
Axes of the slice: x: 4, y: 4, z: 8 (z_hi: 2, z_lo: 4; z = z_hi * 4 + z_lo), core: 2. Of those that a mesh axis runs over, the one named last changes fastest.
Arguments:
- tokens: bfloat16 [1024, 4096], P(('dp', 'fsdp')), may hold values from -6 to 6
- cotangent: bfloat16 [1024, 4096], P(('dp', 'fsdp')), may hold values from -2 to 2
- gate_base: bfloat16 [4096, 10240], P(None, 'fsdp'), may hold values from -0.09375 to 0.09375
- up_base: bfloat16 [4096, 10240], P(None, 'fsdp'), may hold values from -0.09375 to 0.09375
- out_base: bfloat16 [10240, 4096], P('fsdp'), may hold values from -0.0625 to 0.0625
- subspace: float32 [512, 128], P('fsdp'), may hold values from -6 to 6
- sign_flips: int32 [2, 512, 128, 640], P(None, 'fsdp'), may hold values from -1 to 1, as said below
- fast_gains: bfloat16 [2, 512, 128, 640], P(None, None, 'fsdp'), may hold values from -5 to 5
- fast_scales: float32 [2, 512, 640], P(None, 'fsdp'), may hold values from 0.5 to 2
- block_orders: int32 [2, 512], replicated, may hold values from 0 to 511, each once within a row
Outputs:
- subspace_grad: float32 [512, 128], P('fsdp')
The draws below stay inside these ranges and needn't reach their ends.
Inputs may be any that keep to these rules, and one draw needn't show every extreme that they name: `sign_flips`: each entry is -1 or +1.
All inputs are finite; a program needn't handle non-finite values.
Results may differ from the reference program's by a relative error of at most 0.017.
Values may be sent and summed in bfloat16 or wider, within the bound.
No kernel may reach another device: no remote copies, remote signals or barrier semaphores. Data moves between devices by JAX's collectives and lax.ppermute only.
A program may use at most 128 MiB of HBM per device.

```python
import math
import jax
import jax.numpy as jnp
from jax import lax

D = 4096
FF = 10240
HB = 128
NB = 512
ROWS = 256
BLOCKS = 640
N_DP = 4
N_FSDP = 64


def draw_sign_flips(key, part):
    key = jax.random.fold_in(key, 7)
    flips = jax.random.randint(key, (2, NB, HB, BLOCKS), 0, 2)
    return (2 * flips - 1).astype(jnp.int32)


def shard_levels(stream_key, shape, split, least, largest):
    loudness, own = 1.0, jax.random.fold_in(stream_key, 6)
    for axis_at, blocks in split:
        heights = jnp.exp(jax.random.uniform(jax.random.fold_in(own, axis_at), (blocks,), jnp.float32, least / len(split), largest / len(split)))
        loudness = loudness * jnp.repeat(heights, shape[axis_at] // blocks).reshape([-1 if axis == axis_at else 1 for axis in range(len(shape))])
    return loudness


def noise(own_key, shape, deviation, limit, pieces=(), kind=jnp.bfloat16):
    entries = deviation * jax.random.normal(own_key, shape, jnp.float32)
    if pieces:
        entries = entries * shard_levels(own_key, shape, pieces, -0.22, 0.18)
    return jnp.clip(entries, -limit, limit).astype(kind)


def setup_inputs(seed: int = 0) -> dict:
    seeds = jax.random.split(jax.random.key(seed), 11)
    return {
        "tokens": noise(seeds[0], (N_DP * ROWS, D), 1.0, 6.0, ((0, 256),)),
        "cotangent": noise(seeds[1], (N_DP * ROWS, D), (4.0 * (N_DP * ROWS) ** -0.5), 2.0, ((0, 256),)),
        "gate_base": noise(seeds[2], (D, FF), D ** -0.5, 0.09375, ((1, 64),)),
        "up_base": noise(seeds[3], (D, FF), D ** -0.5, 0.09375, ((1, 64),)),
        "out_base": noise(seeds[4], (FF, D), FF ** -0.5, 0.0625, ((0, 64),)),
        "subspace": noise(seeds[5], (NB, HB), 1.0, 6.0, ((0, 64),), jnp.float32),
        "sign_flips": draw_sign_flips(jax.random.fold_in(seeds[10], 71), 0),
        "fast_gains": noise(seeds[7], (2, NB, HB, BLOCKS), 1.0, 5.0, ((2, 64),)),
        "fast_scales": jnp.clip(jnp.exp(math.log(2.0) - 1.3862944 * jax.random.uniform(seeds[8], (2, NB, BLOCKS), jnp.float32) ** shard_levels(seeds[8], (2, NB, BLOCKS), ((1, 64),), -0.2, 0.2)), 0.5, 2.0),
        "block_orders": jax.vmap(lambda own: jax.random.permutation(own, NB))(jax.random.split(seeds[9], 2)).reshape((2, NB)).astype(jnp.int32),
    }


def hadamard(size, dtype):
    index = jnp.arange(size, dtype=jnp.int32)
    anded = jnp.bitwise_and(index[:, None], index[None, :])
    parity = jnp.zeros((size, size), jnp.int32)
    for bit in range(max(size.bit_length() - 1, 0)):
        parity = jnp.bitwise_xor(parity, jnp.bitwise_and(jnp.right_shift(anded, bit), 1))
    return (1 - 2 * parity).astype(dtype)


def gelu_tanh(value):
    argument = 0.7978845608028654 * (value + 0.044715 * value * value * value)
    return 0.5 * value * (1.0 + jnp.tanh(argument))


def gelu_slope(value):
    argument = 0.7978845608028654 * (value + 0.044715 * value * value * value)
    tangent = jnp.tanh(argument)
    return 0.5 * (1.0 + tangent) + 0.5 * value * (1.0 - tangent * tangent) * 0.7978845608028654 * (1.0 + 0.134145 * value * value)


def expand(signs, subspace, gains, scales, order, factor, parts):
    nb, hb, blocks = signs.shape
    inner = nb // parts
    highest = lax.Precision.HIGHEST
    lifted = signs.astype(jnp.float32) * subspace[:, :, None]
    grouped = lifted.reshape(parts, inner, hb, blocks)
    grouped = jnp.einsum('dc,pack->padk', hadamard(hb, jnp.float32), grouped, precision=highest)
    grouped = jnp.einsum('ba,pack->pbck', hadamard(inner, jnp.float32), grouped, precision=highest)
    first = (grouped * (inner * hb) ** -0.5).astype(jnp.bfloat16)
    turned = jnp.einsum('qp,pack->qack', hadamard(parts, jnp.float32), first.astype(jnp.float32), precision=highest) * parts ** -0.5
    turned = turned.reshape(nb, hb, blocks)
    mixed = (gains.astype(jnp.float32) * turned[order]).astype(jnp.bfloat16)
    second = jnp.einsum('cb,bxk->cxk', hadamard(nb, jnp.float32), mixed.astype(jnp.float32), precision=highest)
    second = (second * nb ** -0.5).astype(jnp.bfloat16)
    wide = jnp.einsum('dc,bck->bdk', hadamard(hb, jnp.float32), second.astype(jnp.float32), precision=highest)
    return wide * (scales[:, None, :] * (factor * hb ** -0.5))


def adjoint(grads, signs, gains, scales, order, factor, parts):
    nb, hb, blocks = signs.shape
    inner = nb // parts
    highest = lax.Precision.HIGHEST
    scaled = grads * (scales[:, None, :] * (factor * hb ** -0.5))
    back = jnp.einsum('dc,bck->bdk', hadamard(hb, jnp.float32), scaled, precision=highest).astype(jnp.bfloat16)
    spread = jnp.einsum('cb,bxk->cxk', hadamard(nb, jnp.float32), back.astype(jnp.float32), precision=highest) * nb ** -0.5
    spread = (gains.astype(jnp.float32) * spread).astype(jnp.bfloat16)
    inverse = jnp.zeros((nb,), jnp.int32).at[order].set(jnp.arange(nb, dtype=jnp.int32))
    reverted = spread[inverse].reshape(parts, inner, hb, blocks)
    folded = jnp.einsum('qp,pack->qack', hadamard(parts, jnp.float32), reverted.astype(jnp.float32), precision=highest) * parts ** -0.5
    folded = folded.astype(jnp.bfloat16)
    wide = jnp.einsum('dc,pack->padk', hadamard(hb, jnp.float32), folded.astype(jnp.float32), precision=highest)
    wide = jnp.einsum('ba,pack->pbck', hadamard(inner, jnp.float32), wide, precision=highest) * (inner * hb) ** -0.5
    return jnp.sum(signs.astype(jnp.float32) * wide.reshape(nb, hb, blocks), axis=2)


def contract(left, right, left_dim, right_dim):
    return lax.dot_general(left, right, (((left_dim,), (right_dim,)), ((), ())), preferred_element_type=jnp.float32)


def reference(tokens, cotangent, gate_base, up_base, out_base, subspace, sign_flips, fast_gains, fast_scales, block_orders):
    parts = N_FSDP
    factors = (D ** -0.5, FF ** -0.5)
    layout = (NB, HB, BLOCKS)
    delta_gate = expand(sign_flips[0], subspace, fast_gains[0], fast_scales[0], block_orders[0], factors[0], parts)
    delta_out = expand(sign_flips[1], subspace, fast_gains[1], fast_scales[1], block_orders[1], factors[1], parts)
    delta_gate = delta_gate.reshape(parts, D, FF // parts).transpose(1, 0, 2).reshape(D, FF)
    gate_weight = (gate_base + delta_gate).astype(jnp.bfloat16)
    out_weight = (out_base + delta_out.reshape(FF, D)).astype(jnp.bfloat16)
    gate = jnp.dot(tokens, gate_weight, preferred_element_type=jnp.float32)
    up = jnp.dot(tokens, up_base, preferred_element_type=jnp.float32)
    hidden = (gelu_tanh(gate) * up).astype(jnp.bfloat16)
    hidden_grad = contract(cotangent, out_weight, 1, 1)
    gate_grad = (hidden_grad * up * gelu_slope(gate)).astype(jnp.bfloat16)
    out_grad = contract(hidden, cotangent, 0, 0)
    in_grad = contract(tokens, gate_grad, 0, 0)
    in_grad = in_grad.reshape(D, parts, FF // parts).transpose(1, 0, 2).reshape(layout)
    out_grad = out_grad.reshape(layout)
    total = adjoint(in_grad, sign_flips[0], fast_gains[0], fast_scales[0], block_orders[0], factors[0], parts)
    total = total + adjoint(out_grad, sign_flips[1], fast_gains[1], fast_scales[1], block_orders[1], factors[1], parts)
    return total
```

```python
import functools

import jax
import jax.numpy as jnp
import numpy as np
from jax import lax
from jax.experimental import pallas as pl
from jax.experimental.pallas import tpu as pltpu
from jax.sharding import Mesh, PartitionSpec as P

D = 4096
FF = 10240
BF = jnp.bfloat16
F32 = jnp.float32
AXES = ("zh", "co", "y", "x", "zl")
FSDP = ("y", "x", "zl")
HALVES = ("zh", "y", "x", "zl")
VMEM_BYTES = 60 * 1024 * 1024


def sylvester(size):
    matrix = np.ones((1, 1), np.float32)
    while matrix.shape[0] < size:
        matrix = np.block([[matrix, matrix], [matrix, -matrix]])
    return matrix


@functools.cache
def tables():
    h8, h128, h512 = sylvester(8), sylvester(128), sylvester(512)
    lift = np.stack(
        [
            (h128[par::2][:, None, None, :] * h8[None, :, :, None]).reshape(512, 1024)
            for par in range(2)
        ]
    )
    spread = np.stack(
        [
            (h128[:, par::2][None, :, :, None] * np.eye(8)[:, None, None, :]).reshape(1024, 512)
            for par in range(2)
        ]
    )
    turned = spread.reshape(2, 32, 32, 512).transpose(0, 2, 1, 3).reshape(2, 1024, 512)
    out = np.stack([spread, turned])
    back = out.transpose(0, 1, 3, 2)
    hidden = np.arange(160)
    place = (hidden % 5) * 32 + hidden // 5
    window = np.zeros((4, 256, 160), np.float32)
    for q in range(4):
        window[q, 32 * q + hidden, place] = 1
    order = np.zeros((160, 160), np.float32)
    order[place, hidden] = 1
    columns = np.zeros((512, 512), np.float32)
    q, r = np.divmod(np.arange(512), 128)
    columns[np.arange(512), r * 4 + q] = 1
    cast = lambda value: np.ascontiguousarray(value).astype(BF)
    return dict(
        lift=cast(lift),
        land=cast(lift.transpose(0, 2, 1)),
        out=cast(out),
        back=cast(back),
        h512=cast(h512),
        window=cast(window),
        order=cast(order),
        columns=cast(columns),
    )


def dot(left, right):
    return jnp.dot(left, right, preferred_element_type=F32)


def dot_t(left, right):
    return lax.dot_general(left, right, (((1,), (1,)), ((), ())), preferred_element_type=F32)


def dot_l(left, right):
    return lax.dot_general(left, right, (((0,), (0,)), ((), ())), preferred_element_type=F32)


def params():
    return pltpu.CompilerParams(vmem_limit_bytes=VMEM_BYTES)


def lift_kernel(place, sub, signs, table, out, total):
    step = pl.program_id(0)
    row = jnp.concatenate([sub[pl.ds(2 * step, 1), :], sub[pl.ds(2 * step + 1, 1), :]], axis=1)
    high = row.astype(BF)
    low = (row - high.astype(F32)).astype(BF)
    flips = signs[0].astype(F32).astype(BF)
    part = dot(table[0] * high, flips) + dot(table[0] * low, flips)

    @pl.when(step == 0)
    def _():
        total[...] = part

    @pl.when(step > 0)
    def _():
        total[...] += part

    @pl.when(step == 3)
    def _():
        out[...] = (total[...] * (1.0 / 32.0)).astype(BF)


def lift_call(place, subspace, signs, table):
    return pl.pallas_call(
        lift_kernel,
        out_shape=jax.ShapeDtypeStruct((512, 640), BF),
        grid_spec=pltpu.PrefetchScalarGridSpec(
            num_scalar_prefetch=1,
            grid=(4,),
            in_specs=[
                pl.BlockSpec((8, 128), lambda i, s: (0, 0)),
                pl.BlockSpec((1, 256, 640), lambda i, s: (s[0], i, 0)),
                pl.BlockSpec((1, 512, 256), lambda i, s: (s[1], 0, i)),
            ],
            out_specs=pl.BlockSpec((512, 640), lambda i, s: (0, 0)),
            scratch_shapes=[pltpu.VMEM((512, 640), F32)],
        ),
        compiler_params=params(),
        name="lift",
    )(place, subspace, signs, table)


def middle_kernel(mixer, gains, h512, first, *rest):
    out = rest[-1]
    turned = dot(mixer[...], first[...]) * 0.125
    mixed = (gains[...].astype(F32) * turned).astype(BF)
    second = (dot(h512[...], mixed) * 512**-0.5).astype(BF)
    out[0] = second
    out[1] = second


def middle_call(mixer, gains, h512, first, after=()):
    whole = pl.BlockSpec(memory_space=pltpu.VMEM)
    away = pl.BlockSpec(memory_space=pl.ANY)
    return pl.pallas_call(
        middle_kernel,
        out_shape=jax.ShapeDtypeStruct((2, 512, 640), BF),
        in_specs=[whole] * 4 + [away] * len(after),
        out_specs=whole,
        compiler_params=params(),
        name="middle",
    )(mixer, gains, h512, first, *after)


def revert_kernel(mixer, gains, h512, backs, out):
    spread = (dot(h512[...], backs[0]) + dot(h512[...], backs[1])) * 512**-0.5
    spread = (gains[...].astype(F32) * spread).astype(BF)
    out[...] = (dot(mixer[...], spread) * 0.125).astype(BF)


def revert_call(mixer, gains, h512, backs):
    return pl.pallas_call(
        revert_kernel,
        out_shape=jax.ShapeDtypeStruct((512, 640), BF),
        compiler_params=params(),
        name="revert",
    )(mixer, gains, h512, backs)


def land_kernel(place, signs, table, folded, out):
    step = pl.program_id(0)
    wide = dot(table[0], folded[...]) * signs[0].astype(F32)
    lanes = wide[:, 0:128]
    for tile in range(1, 5):
        lanes = lanes + wide[:, tile * 128 : (tile + 1) * 128]
    for block in range(2):
        columns = jnp.transpose(lanes[block * 128 : (block + 1) * 128, :])
        out[pl.ds(2 * step + block, 1), :] = jnp.sum(columns, axis=0, keepdims=True) * (1.0 / 32.0)


def land_call(place, signs, table, folded):
    return pl.pallas_call(
        land_kernel,
        out_shape=jax.ShapeDtypeStruct((8, 128), F32),
        grid_spec=pltpu.PrefetchScalarGridSpec(
            num_scalar_prefetch=1,
            grid=(4,),
            in_specs=[
                pl.BlockSpec((1, 256, 640), lambda i, s: (s[0], i, 0)),
                pl.BlockSpec((1, 256, 512), lambda i, s: (s[1], i, 0)),
                pl.BlockSpec((512, 640), lambda i, s: (0, 0)),
            ],
            out_specs=pl.BlockSpec((8, 128), lambda i, s: (0, 0)),
        ),
        compiler_params=params(),
        name="land",
    )(place, signs, table, folded)


def base_kernel(*refs):
    left, right = refs[0:4], refs[4:8]
    gate_base, up_base, out_base, order, columns = refs[8:13]
    x_cols, x_rows, dy, gate, up, grad = refs[13:19]
    x, sems = refs[19:21]
    copies = []
    for i in range(4):
        copies.append(pltpu.make_async_copy(left[i], x.at[pl.ds(64 * i, 64)], sems.at[len(copies)]))
    for i in range(4):
        for j in range(4):
            copies.append(
                pltpu.make_async_copy(
                    right[i].at[pl.ds(16 * j, 16)],
                    dy.at[pl.ds(64 * j + 16 * i, 16)],
                    sems.at[len(copies)],
                )
            )
    for copy in copies:
        copy.start()
    ordered = [dot(order[...], item[...]).astype(BF) for item in (gate_base, up_base, out_base)]
    for copy in copies:
        copy.wait()
    gate[...] = dot_t(x[...], ordered[0])
    up[...] = dot_t(x[...], ordered[1])
    grad[...] = dot_t(dy[...], ordered[2])
    for g in range(8):
        part = x[:, g * 512 : (g + 1) * 512]
        wide = dot_t(part, columns[...]).astype(BF)
        tall = dot_t(columns[...], part).astype(BF)
        for q in range(4):
            at = q * 1024 + g * 128
            x_cols[:, at : at + 128] = wide[:, q * 128 : (q + 1) * 128]
            x_rows[at : at + 128, :] = tall[q * 128 : (q + 1) * 128, :]


def base_call(left, right, gate_base, up_base, out_base, order, columns):
    whole = pl.BlockSpec(memory_space=pltpu.VMEM)
    away = pl.BlockSpec(memory_space=pl.ANY)
    return pl.pallas_call(
        base_kernel,
        out_shape=[
            jax.ShapeDtypeStruct((256, 4096), BF),
            jax.ShapeDtypeStruct((4096, 256), BF),
            jax.ShapeDtypeStruct((256, 4096), BF),
            jax.ShapeDtypeStruct((256, 160), F32),
            jax.ShapeDtypeStruct((256, 160), F32),
            jax.ShapeDtypeStruct((256, 160), F32),
        ],
        in_specs=[away] * 8 + [whole] * 5,
        out_specs=[whole] * 6,
        scratch_shapes=[pltpu.VMEM((256, 4096), BF), pltpu.SemaphoreType.DMA((20,))],
        compiler_params=params(),
        name="base",
    )(*left, *right, gate_base, up_base, out_base, order, columns)


def layer_kernel(
    place,
    own,
    other,
    out_table,
    back_table,
    scales0,
    scales1,
    window,
    x_cols,
    x_rows,
    dy,
    gate_part,
    up_part,
    grad_part,
    keep,
    send,
    e0,
    w1,
    g0,
    g1,
):
    mine = place[1]
    theirs = 1 - mine
    c0 = (D**-0.5) * (128**-0.5)
    c1 = (FF**-0.5) * (128**-0.5)
    for i in range(4):
        rows = pl.ds(256 * i, 256)
        wide = dot(out_table[0, mine, rows, :], own[0]) + dot(out_table[0, theirs, rows, :], other[0])
        for j in range(2):
            b = 2 * i + j
            e0[128 * b : 128 * (b + 1), :] = (
                wide[128 * j : 128 * (j + 1), :] * (scales0[b : b + 1, :] * c0)
            ).astype(BF)
    scale1 = scales1[...] * c1
    for i in range(4):
        rows = pl.ds(256 * i, 256)
        wide = dot(out_table[1, mine, rows, :], own[1]) + dot(out_table[1, theirs, rows, :], other[1])
        for j in range(8):
            w = 8 * i + j
            piece = (wide[32 * j : 32 * (j + 1), :] * scale1).astype(BF)
            for kt in range(5):
                v, jt = divmod(5 * w + kt, 32)
                w1[32 * v : 32 * (v + 1), 128 * jt : 128 * (jt + 1)] = piece[:, 128 * kt : 128 * (kt + 1)]
    gate = gate_part[...]
    for q in range(4):
        part = dot(x_cols[:, 1024 * q : 1024 * (q + 1)], e0[:, 128 * q : 128 * q + 256])
        high = part.astype(BF)
        low = (part - high.astype(F32)).astype(BF)
        gate = gate + dot(high, window[q]) + dot(low, window[q])
    up = up_part[...]
    grad = grad_part[...] + dot_t(dy[...], w1[...])
    argument = 0.7978845608028654 * (gate + 0.044715 * gate * gate * gate)
    tangent = jnp.tanh(argument)
    half = 0.5 * (1.0 + tangent)
    hidden = (gate * half * up).astype(BF)
    slope = half + 0.5 * gate * (1.0 - tangent * tangent) * 0.7978845608028654 * (
        1.0 + 0.134145 * gate * gate
    )
    gate_grad = (grad * up * slope).astype(BF)
    out_grad = dot_l(hidden, dy[...])
    for w in range(32):
        for kt in range(5):
            v, jt = divmod(5 * w + kt, 32)
            tile = slice(128 * kt, 128 * (kt + 1))
            g1[32 * w : 32 * (w + 1), tile] = (
                out_grad[32 * v : 32 * (v + 1), 128 * jt : 128 * (jt + 1)] * scale1[:, tile]
            ).astype(BF)
    keep[1] = dot(back_table[1, mine], g1[...]).astype(BF)
    send[1] = dot(back_table[1, theirs], g1[...]).astype(BF)
    windows = [dot_t(gate_grad, window[q]).astype(BF) for q in range(4)]
    for i in range(4):
        parts = [dot(x_rows[1024 * q + 256 * i : 1024 * q + 256 * (i + 1), :], windows[q]) for q in range(4)]
        tiles = [parts[0][:, 0:128]]
        for q in range(3):
            tiles.append(parts[q][:, 128:256] + parts[q + 1][:, 0:128])
        tiles.append(parts[3][:, 128:256])
        for j in range(2):
            b = 2 * i + j
            for kt in range(5):
                tile = slice(128 * kt, 128 * (kt + 1))
                g0[128 * b : 128 * (b + 1), tile] = (
                    tiles[kt][128 * j : 128 * (j + 1), :] * (scales0[b : b + 1, tile] * c0)
                ).astype(BF)
    keep[0] = dot(back_table[0, mine], g0[...]).astype(BF)
    send[0] = dot(back_table[0, theirs], g0[...]).astype(BF)


def layer_call(place, *args):
    whole = pl.BlockSpec(memory_space=pltpu.VMEM)
    return pl.pallas_call(
        layer_kernel,
        out_shape=[jax.ShapeDtypeStruct((2, 512, 640), BF)] * 2,
        in_specs=[pl.BlockSpec(memory_space=pltpu.SMEM)] + [whole] * len(args),
        out_specs=[whole] * 2,
        scratch_shapes=[
            pltpu.VMEM((1024, 640), BF),
            pltpu.VMEM((160, 4096), BF),
            pltpu.VMEM((1024, 640), BF),
            pltpu.VMEM((1024, 640), BF),
        ],
        compiler_params=params(),
        name="layer",
    )(place, *args)


def shifted(item, axis):
    return [item] + [
        lax.ppermute(item, axis, [(i, (i + by) % 4) for i in range(4)]) for by in (1, 2, 3)
    ]


def swap_core(item):
    return lax.ppermute(item, "co", [(0, 1), (1, 0)])


def mixers(order):
    block = jnp.arange(512, dtype=jnp.int32)

    def build(left, right):
        both = (left >> 3) & (right >> 3)
        both = both ^ (both >> 4)
        both = both ^ (both >> 2)
        both = both ^ (both >> 1)
        sign = 1 - 2 * (both & 1)
        return jnp.where((left & 7) == (right & 7), sign, 0).astype(BF)

    return build(order[:, None], block[None, :]), build(block[:, None], order[None, :])


def on_device(
    tokens,
    cotangent,
    gate_base,
    up_base,
    out_base,
    subspace,
    sign_flips,
    fast_gains,
    fast_scales,
    block_orders,
):
    const = tables()
    which, core = lax.axis_index("zh"), lax.axis_index("co")
    place = jnp.stack([which, core]).astype(jnp.int32)
    signs = sign_flips.reshape(2, 1024, 640)

    both, place = lax.optimization_barrier((jnp.concatenate([tokens, cotangent], axis=0), place))
    slots = shifted(both, "zl")
    left = jnp.concatenate([slot[:4] for slot in slots], axis=0)
    right = jnp.concatenate([slot[4:] for slot in slots], axis=0)
    left = jnp.concatenate(shifted(left, "x"), axis=0)
    right = jnp.concatenate(shifted(right, "y"), axis=0)
    stage = (left, right)
    left, right = shifted(left, "y"), shifted(right, "x")

    first = lift_call(place, subspace, signs, const["lift"])
    first = lax.all_to_all(first.reshape(64, 8, 640), FSDP, split_axis=0, concat_axis=0, tiled=True)

    order = lax.dynamic_index_in_dim(block_orders, which, 0, keepdims=False)
    forward, adjoint = mixers(order)
    gains = lax.dynamic_slice(fast_gains, (which, 0, core, 0), (1, 512, 1, 640)).reshape(512, 640)
    h512 = const["h512"]
    second = middle_call(forward, gains, h512, first.reshape(512, 640), stage)
    second = lax.all_to_all(
        second.reshape(128, 8, 640), HALVES, split_axis=0, concat_axis=0, tiled=True
    ).reshape(2, 512, 640)

    prepared = base_call(
        left, right, gate_base.T, up_base.T, out_base, const["order"], const["columns"]
    )
    second, *prepared = lax.optimization_barrier((second, *prepared))
    other = swap_core(second)
    keep, send = layer_call(
        place,
        second,
        other,
        const["out"],
        const["back"],
        fast_scales[0],
        jnp.repeat(fast_scales[1], 4, axis=0),
        const["window"],
        *prepared,
    )
    backs = (keep.astype(F32) + swap_core(send).astype(F32)).astype(BF)
    backs = lax.all_to_all(
        backs.reshape(128, 8, 640), HALVES, split_axis=0, concat_axis=0, tiled=True
    ).reshape(2, 512, 640)
    folded = revert_call(adjoint, gains, h512, backs)
    folded = lax.all_to_all(
        folded.reshape(64, 8, 640), FSDP, split_axis=0, concat_axis=0, tiled=True
    )
    part = land_call(place, signs, const["land"], folded.reshape(512, 640))
    for axis in ("co", "zh"):
        part = part + lax.ppermute(part, axis, [(0, 1), (1, 0)])
    return part


def solution(mesh):
    split = Mesh(mesh.devices.reshape(2, 2, 4, 4, 4), AXES)
    group = ("zh", "co")
    in_specs = (
        P(group + FSDP, None),
        P(group + FSDP, None),
        P(None, FSDP),
        P(None, FSDP),
        P(FSDP, None),
        P(FSDP, None),
        P(None, FSDP, None, None),
        P(None, None, FSDP, None),
        P(None, FSDP, None),
        P(),
    )
    return jax.shard_map(
        on_device, mesh=split, in_specs=in_specs, out_specs=P(FSDP, None), check_vma=False
    )
```

```python
import functools

import jax
import jax.numpy as jnp
import numpy as np
from jax import lax
from jax.experimental import pallas as pl
from jax.experimental.pallas import tpu as pltpu
from jax.sharding import Mesh, PartitionSpec as P

D = 4096
FF = 10240
BF = jnp.bfloat16
F32 = jnp.float32
AXES = ("zh", "co", "y", "x", "zl")
FSDP = ("y", "x", "zl")
HALVES = ("zh", "y", "x", "zl")
VMEM_BYTES = 60 * 1024 * 1024


def sylvester(size):
    matrix = np.ones((1, 1), np.float32)
    while matrix.shape[0] < size:
        matrix = np.block([[matrix, matrix], [matrix, -matrix]])
    return matrix


@functools.cache
def tables():
    h128, h512 = sylvester(128), sylvester(512)
    half = np.stack([h128[par::2] for par in range(2)])
    pair = np.stack([np.concatenate([h128[:, par::2], h128[:, 1 - par :: 2]], 1) for par in range(2)])
    hidden = np.arange(160)
    place = (hidden % 5) * 32 + hidden // 5
    window = np.zeros((4, 256, 160), np.float32)
    for q in range(4):
        window[q, 32 * q + hidden, place] = 1
    order = np.zeros((160, 160), np.float32)
    order[place, hidden] = 1
    columns = np.zeros((512, 512), np.float32)
    q, r = np.divmod(np.arange(512), 128)
    columns[np.arange(512), r * 4 + q] = 1
    apart = np.zeros((32, 32), np.float32)
    row = np.arange(16)
    apart[row, (row // 4) * 8 + row % 4] = 1
    apart[16 + row, (row // 4) * 8 + 4 + row % 4] = 1
    cast = lambda value: np.ascontiguousarray(value).astype(BF)
    return dict(
        half=cast(half),
        half_t=cast(half.transpose(0, 2, 1)),
        pair=cast(pair),
        pair_t=cast(pair.transpose(0, 2, 1)),
        h512=cast(h512),
        window=cast(window),
        order=cast(order),
        columns=cast(columns),
        apart=cast(apart),
        unit=cast(np.eye(256)),
    )


def butterfly(items):
    step = 1
    while step < len(items):
        items = [
            items[i] + items[i ^ step] if not i & step else items[i ^ step] - items[i]
            for i in range(len(items))
        ]
        step *= 2
    return items


def dot(left, right):
    return jnp.dot(left, right, preferred_element_type=F32)


def dot_t(left, right):
    return lax.dot_general(left, right, (((1,), (1,)), ((), ())), preferred_element_type=F32)


def dot_l(left, right):
    return lax.dot_general(left, right, (((0,), (0,)), ((), ())), preferred_element_type=F32)


def params():
    return pltpu.CompilerParams(vmem_limit_bytes=VMEM_BYTES)


def lift_kernel(place, sub, signs, half, out, flips, parts, rows, sems):
    copies = []
    for a in range(8):
        block = pl.ds(128 * a, 128)
        copies.append(pltpu.make_async_copy(signs.at[place[0], block], flips.at[block], sems.at[a]))
        copies[-1].start()
    grid = half[place[1]]
    for a in range(8):
        row = sub[a : a + 1, :]
        high = row.astype(BF)
        low = (row - high.astype(F32)).astype(BF)
        scaled = jnp.concatenate([grid * high, grid * low], axis=1)
        copies[a].wait()
        flip = flips[128 * a : 128 * (a + 1), :].astype(F32).astype(BF)
        parts[a] = dot(scaled, jnp.concatenate([flip, flip], axis=0))
    for kt in range(5):
        tile = slice(128 * kt, 128 * (kt + 1))
        for part in range(4):
            at = slice(16 * part, 16 * (part + 1))
            mixed = butterfly([parts[a, at, tile] for a in range(8)])
            for b in range(8):
                rows[kt, pl.ds(128 * part + b, 16, stride=8), :] = mixed[b]
    for kt in range(5):
        out[:, 128 * kt : 128 * (kt + 1)] = (rows[kt] * (1.0 / 32.0)).astype(BF)


def lift_call(place, subspace, signs, half):
    whole = pl.BlockSpec(memory_space=pltpu.VMEM)
    away = pl.BlockSpec(memory_space=pl.ANY)
    return pl.pallas_call(
        lift_kernel,
        out_shape=jax.ShapeDtypeStruct((512, 640), BF),
        in_specs=[pl.BlockSpec(memory_space=pltpu.SMEM), whole, away, whole],
        out_specs=whole,
        scratch_shapes=[
            pltpu.VMEM((1024, 640), jnp.int32),
            pltpu.VMEM((8, 64, 640), F32),
            pltpu.VMEM((5, 512, 128), F32),
            pltpu.SemaphoreType.DMA((8,)),
        ],
        compiler_params=params(),
        name="lift",
    )(place, subspace, signs, half)


def middle_kernel(mixer, gains, h512, first, *rest):
    out = rest[-1]
    turned = dot(mixer[...], first[...]) * 0.125
    mixed = (gains[...].astype(F32) * turned).astype(BF)
    second = (dot(h512[...], mixed) * 512**-0.5).astype(BF)
    out[0] = second
    out[1] = second


def middle_call(mixer, gains, h512, first, after=()):
    whole = pl.BlockSpec(memory_space=pltpu.VMEM)
    away = pl.BlockSpec(memory_space=pl.ANY)
    return pl.pallas_call(
        middle_kernel,
        out_shape=jax.ShapeDtypeStruct((2, 512, 640), BF),
        in_specs=[whole] * 4 + [away] * len(after),
        out_specs=whole,
        compiler_params=params(),
        name="middle",
    )(mixer, gains, h512, first, *after)


def revert_kernel(mixer, gains, h512, backs, out):
    spread = (dot(h512[...], backs[0]) + dot(h512[...], backs[1])) * 512**-0.5
    spread = (gains[...].astype(F32) * spread).astype(BF)
    out[...] = (dot(mixer[...], spread) * 0.125).astype(BF)


def revert_call(mixer, gains, h512, backs):
    return pl.pallas_call(
        revert_kernel,
        out_shape=jax.ShapeDtypeStruct((512, 640), BF),
        compiler_params=params(),
        name="revert",
    )(mixer, gains, h512, backs)


def land_kernel(place, signs, half_t, folded, out, flips, rows, parts, sems):
    copies = []
    for a in range(8):
        block = pl.ds(128 * a, 128)
        copies.append(pltpu.make_async_copy(signs.at[place[0], block], flips.at[block], sems.at[a]))
        copies[-1].start()
    grid = half_t[place[1]]
    for kt in range(5):
        rows[kt] = folded[:, 128 * kt : 128 * (kt + 1)].astype(F32)
    for a in range(8):
        block = [rows[kt, pl.ds(a, 64, stride=8), :] for kt in range(5)]
        parts[a] = dot(grid, jnp.concatenate(block, axis=1).astype(BF))
    for copy in copies:
        copy.wait()
    ones = jnp.ones((8, 128), BF)
    for part in range(8):
        at = slice(16 * part, 16 * (part + 1))
        lanes = [None] * 8
        for kt in range(5):
            tile = slice(128 * kt, 128 * (kt + 1))
            mixed = butterfly([parts[a, at, tile] for a in range(8)])
            for b in range(8):
                start = 128 * b + 16 * part
                term = mixed[b] * flips[start : start + 16, tile].astype(F32)
                lanes[b] = term if lanes[b] is None else lanes[b] + term
        for b in range(8):
            parts[b, at, 0:128] = lanes[b]
    for b in range(8):
        full = parts[b, :, 0:128]
        high = full.astype(BF)
        rest = full - high.astype(F32)
        low = rest.astype(BF)
        last = (rest - low.astype(F32)).astype(BF)
        sums = dot_t(ones, high) + dot_t(ones, low) + dot_t(ones, last)
        out[b : b + 1, :] = sums[0:1, :] * (1.0 / 32.0)


def land_call(place, signs, half_t, folded):
    whole = pl.BlockSpec(memory_space=pltpu.VMEM)
    away = pl.BlockSpec(memory_space=pl.ANY)
    return pl.pallas_call(
        land_kernel,
        out_shape=jax.ShapeDtypeStruct((8, 128), F32),
        in_specs=[pl.BlockSpec(memory_space=pltpu.SMEM), away, whole, whole],
        out_specs=whole,
        scratch_shapes=[
            pltpu.VMEM((1024, 640), jnp.int32),
            pltpu.VMEM((5, 512, 128), F32),
            pltpu.VMEM((8, 128, 640), F32),
            pltpu.SemaphoreType.DMA((8,)),
        ],
        compiler_params=params(),
        name="land",
    )(place, signs, half_t, folded)


def sort_columns(item, columns, target):
    height = item.shape[0]
    stack = jnp.concatenate([item[:, 512 * g : 512 * (g + 1)] for g in range(8)], axis=0)
    stack = dot_t(stack, columns).astype(BF)
    for g in range(8):
        for q in range(4):
            at = 1024 * q + 128 * g
            target[:, at : at + 128] = stack[height * g : height * (g + 1), 128 * q : 128 * (q + 1)]


def part_kernel(a, b, c, d, order, columns, left, right):
    stack = jnp.concatenate([item[...].astype(F32) for item in (a, b, c, d)], axis=0).astype(BF)
    apart = dot(order[...], stack).astype(BF)
    sort_columns(apart[0:16, :], columns[...], left)
    right[...] = apart[16:32, :]


def part_call(slots, order, columns):
    return pl.pallas_call(
        part_kernel,
        out_shape=[jax.ShapeDtypeStruct((16, 4096), BF)] * 2,
        compiler_params=params(),
        name="part",
    )(*slots, order, columns)


def join_kernel(*refs):
    ins, outs = refs[:8], refs[8:10]
    for i in range(8):
        outs[i // 4][16 * (i % 4) : 16 * (i % 4) + 16, :] = ins[i][...]


def join_call(left, right):
    return pl.pallas_call(
        join_kernel,
        out_shape=[jax.ShapeDtypeStruct((64, 4096), BF)] * 2,
        compiler_params=params(),
        name="join",
    )(*left, *right)


def sort_kernel(gate_base, up_base, out_base, order, columns, gate, up, out):
    out[...] = dot(order[...], out_base[...]).astype(BF)
    for base, target in ((gate_base, gate), (up_base, up)):
        sort_columns(dot(order[...], base[...]).astype(BF), columns[...], target)


def sort_call(*args):
    return pl.pallas_call(
        sort_kernel,
        out_shape=[jax.ShapeDtypeStruct((160, 4096), BF)] * 3,
        compiler_params=params(),
        name="sort",
    )(*args)


def collect(left, right, x, dy, sems):
    copies = [pltpu.make_async_copy(left[i], x.at[pl.ds(64 * i, 64)], sems.at[i]) for i in range(4)]
    late = [
        pltpu.make_async_copy(
            right[i].at[pl.ds(16 * j, 16)], dy.at[pl.ds(64 * j + 16 * i, 16)], sems.at[4 + 4 * i + j]
        )
        for i in range(4)
        for j in range(4)
    ]
    for copy in copies + late:
        copy.start()
    return copies, late


def base_kernel(*refs):
    left, right = refs[0:4], refs[4:8]
    gate_base, up_base, out_base, unit = refs[8:12]
    x_rows, gate, up, grad = refs[12:16]
    x, dy, sems = refs[16:19]
    first, late = collect(left, right, x, dy, sems)
    for copy in first:
        copy.wait()
    gate[...] = dot_t(x[...], gate_base[...])
    up[...] = dot_t(x[...], up_base[...])
    for g in range(16):
        at = slice(256 * g, 256 * (g + 1))
        x_rows[at, :] = dot_t(unit[...], x[:, at]).astype(BF)
    for copy in late:
        copy.wait()
    grad[...] = dot_t(dy[...], out_base[...])


COST = 2 * 10**10


def base_call(left, right, gate_base, up_base, out_base, unit):
    whole = pl.BlockSpec(memory_space=pltpu.VMEM)
    away = pl.BlockSpec(memory_space=pl.ANY)
    return pl.pallas_call(
        base_kernel,
        out_shape=[jax.ShapeDtypeStruct((4096, 256), BF)]
        + [jax.ShapeDtypeStruct((256, 160), F32)] * 3,
        in_specs=[away] * 8 + [whole] * 4,
        out_specs=[whole] * 4,
        scratch_shapes=[
            pltpu.VMEM((256, 4096), BF),
            pltpu.VMEM((256, 4096), BF),
            pltpu.SemaphoreType.DMA((20,)),
        ],
        compiler_params=params(),
        cost_estimate=pl.CostEstimate(flops=COST, bytes_accessed=10**6, transcendentals=0),
        name="base",
    )(*left, *right, gate_base, up_base, out_base, unit)


def layer_kernel(
    place,
    own_far,
    other_far,
    l0,
    l1,
    l2,
    l3,
    r0,
    r1,
    r2,
    r3,
    x_rows_far,
    pair,
    pair_t,
    scales,
    window,
    gate_part,
    up_part,
    grad_part,
    keep_far,
    send_far,
    own,
    other,
    x_cols,
    x_rows,
    dy,
    near,
    tall,
    e0,
    w1,
    keep,
    send,
    sems,
    piece_sems,
):
    mine = place[1]
    count = [0]
    waits = {}

    def bring(key, source, target):
        copy = pltpu.make_async_copy(source, target, sems.at[count[0]])
        count[0] += 1
        copy.start()
        waits[key] = copy

    for m in range(2):
        bring(("own", m), own_far.at[m], own.at[m])
        bring(("other", m), other_far.at[m], other.at[m])
    first, late = collect((l0, l1, l2, l3), (r0, r1, r2, r3), x_cols, dy, piece_sems)
    bring("x_rows", x_rows_far, x_rows)

    factors = ((D**-0.5) * (128**-0.5), (FF**-0.5) * (128**-0.5))
    tiles = [slice(128 * kt, 128 * (kt + 1)) for kt in range(5)]
    grid, grid_t = pair[mine], pair_t[mine]

    def widen(m, put):
        waits[("own", m)].wait()
        waits[("other", m)].wait()
        for kt in range(5):
            near[0, kt] = own[m, :, tiles[kt]].astype(F32)
            near[1, kt] = other[m, :, tiles[kt]].astype(F32)
        for b in range(8):
            block = jnp.concatenate(
                [
                    jnp.concatenate(
                        [near[side, kt, pl.ds(b, 64, stride=8), :] for kt in range(5)], axis=1
                    )
                    for side in range(2)
                ],
                axis=0,
            ).astype(BF)
            put(b, dot(grid, block) * (scales[m, b : b + 1, :] * factors[m]))

    def put0(b, wide):
        e0[128 * b : 128 * (b + 1), :] = wide.astype(BF)

    def put1(b, wide):
        for kt in range(5):
            tall[kt, 128 * b : 128 * (b + 1), :] = wide[:, tiles[kt]]

    widen(0, put0)
    for copy in first + late + [waits["x_rows"]]:
        copy.wait()
    widen(1, put1)
    for w in range(32):
        for kt in range(5):
            v, jt = divmod(5 * w + kt, 32)
            w1[32 * v : 32 * (v + 1), 128 * jt : 128 * (jt + 1)] = tall[
                kt, pl.ds(w, 32, stride=32), :
            ].astype(BF)
    gate = gate_part[...]
    for q in range(4):
        part = dot(x_cols[:, 1024 * q : 1024 * (q + 1)], e0[:, 128 * q : 128 * q + 256])
        high = part.astype(BF)
        low = (part - high.astype(F32)).astype(BF)
        gate = gate + dot(high, window[q]) + dot(low, window[q])
    up = up_part[...]
    grad = grad_part[...] + dot_t(dy[...], w1[...])
    argument = 0.7978845608028654 * (gate + 0.044715 * gate * gate * gate)
    tangent = jnp.tanh(argument)
    half = 0.5 * (1.0 + tangent)
    hidden = (gate * half * up).astype(BF)
    slope = half + 0.5 * gate * (1.0 - tangent * tangent) * 0.7978845608028654 * (
        1.0 + 0.134145 * gate * gate
    )
    gate_grad = (grad * up * slope).astype(BF)
    out_grad = dot_l(hidden, dy[...])
    for w in range(32):
        for kt in range(5):
            v, jt = divmod(5 * w + kt, 32)
            tall[kt, pl.ds(w, 32, stride=32), :] = out_grad[
                32 * v : 32 * (v + 1), 128 * jt : 128 * (jt + 1)
            ]

    def leave(m, get):
        for b in range(8):
            back = dot(grid_t, (get(b) * (scales[m, b : b + 1, :] * factors[m])).astype(BF))
            for kt in range(5):
                near[0, kt, pl.ds(b, 64, stride=8), :] = back[0:64, tiles[kt]]
                near[1, kt, pl.ds(b, 64, stride=8), :] = back[64:128, tiles[kt]]
        for kt in range(5):
            send[m, :, tiles[kt]] = near[1, kt].astype(BF)
            keep[m, :, tiles[kt]] = near[0, kt].astype(BF)
        bring(("send", m), send.at[m], send_far.at[m])
        bring(("keep", m), keep.at[m], keep_far.at[m])

    def rows_of(b):
        return jnp.concatenate([tall[kt, 128 * b : 128 * (b + 1), :] for kt in range(5)], axis=1)

    leave(1, rows_of)
    windows = [dot_t(gate_grad, window[q]).astype(BF) for q in range(4)]

    for q in range(4):
        part = dot(x_rows[1024 * q : 1024 * (q + 1), :], windows[q])
        tall[q] = part[:, 0:128] + tall[q] if q else part[:, 0:128]
        tall[q + 1] = part[:, 128:256]

    leave(0, rows_of)
    for m in range(2):
        for side in ("send", "keep"):
            waits[(side, m)].wait()


def layer_call(place, own, other, left, right, x_rows, *args):
    whole = pl.BlockSpec(memory_space=pltpu.VMEM)
    away = pl.BlockSpec(memory_space=pl.ANY)
    return pl.pallas_call(
        layer_kernel,
        out_shape=[jax.ShapeDtypeStruct((2, 512, 640), BF)] * 2,
        in_specs=[pl.BlockSpec(memory_space=pltpu.SMEM)] + [away] * 11 + [whole] * len(args),
        out_specs=[away] * 2,
        scratch_shapes=[
            pltpu.VMEM((2, 512, 640), BF),
            pltpu.VMEM((2, 512, 640), BF),
            pltpu.VMEM((256, 4096), BF),
            pltpu.VMEM((4096, 256), BF),
            pltpu.VMEM((256, 4096), BF),
            pltpu.VMEM((2, 5, 512, 128), F32),
            pltpu.VMEM((5, 1024, 128), F32),
            pltpu.VMEM((1024, 640), BF),
            pltpu.VMEM((160, 4096), BF),
            pltpu.VMEM((2, 512, 640), BF),
            pltpu.VMEM((2, 512, 640), BF),
            pltpu.SemaphoreType.DMA((9,)),
            pltpu.SemaphoreType.DMA((20,)),
        ],
        compiler_params=params(),
        name="layer",
    )(place, own, other, *left, *right, x_rows, *args)


def shifted(item, axis):
    return [item] + [
        lax.ppermute(item, axis, [(i, (i + by) % 4) for i in range(4)]) for by in (1, 2, 3)
    ]


def near_two(item, axis):
    return [lax.ppermute(item, axis, [(i, (i + by) % 4) for i in range(4)]) for by in (1, 3)]


def across(back, axis):
    return lax.ppermute(back, axis, [(i, (i + 1) % 4) for i in range(4)])


def ringed(item, axis):
    back, ahead = near_two(item, axis)
    return [item, back, across(back, axis), ahead]


def swap_core(item):
    return lax.ppermute(item, "co", [(0, 1), (1, 0)])


def mixers(order):
    block = jnp.arange(512, dtype=jnp.int32)

    def build(left, right):
        both = (left >> 3) & (right >> 3)
        both = both ^ (both >> 4)
        both = both ^ (both >> 2)
        both = both ^ (both >> 1)
        sign = 1 - 2 * (both & 1)
        return jnp.where((left & 7) == (right & 7), sign, 0).astype(BF)

    return build(order[:, None], block[None, :]), build(block[:, None], order[None, :])


def on_device(
    tokens,
    cotangent,
    gate_base,
    up_base,
    out_base,
    subspace,
    sign_flips,
    fast_gains,
    fast_scales,
    block_orders,
):
    const = tables()
    which, core = lax.axis_index("zh"), lax.axis_index("co")
    place = jnp.stack([which, core]).astype(jnp.int32)
    signs = sign_flips.reshape(2, 1024, 640)

    both, place = lax.optimization_barrier((jnp.concatenate([tokens, cotangent], axis=0), place))
    slots = shifted(both, "zl")
    first = lift_call(place, subspace, signs, const["half"])
    left, right = part_call(slots, const["apart"], const["columns"])
    first, left, right = lax.optimization_barrier((first, left, right))
    left, right = join_call(ringed(left, "x"), ringed(right, "y"))
    stage = (left, right)
    left_near, right_near = near_two(left, "y"), near_two(right, "x")
    first = lax.all_to_all(first.reshape(64, 8, 640), FSDP, split_axis=0, concat_axis=0, tiled=True)

    order = lax.dynamic_index_in_dim(block_orders, which, 0, keepdims=False)
    forward, adjoint = mixers(order)
    gains = lax.dynamic_slice(fast_gains, (which, 0, core, 0), (1, 512, 1, 640)).reshape(512, 640)
    h512 = const["h512"]
    second = middle_call(forward, gains, h512, first.reshape(512, 640), stage)
    _, left_near, right_near, bases = lax.optimization_barrier(
        (second, left_near, right_near, (gate_base.T, up_base.T, out_base))
    )
    second = lax.all_to_all(
        second.reshape(128, 8, 640), HALVES, split_axis=0, concat_axis=0, tiled=True
    ).reshape(2, 512, 640)
    left = [left, left_near[0], across(left_near[0], "y"), left_near[1]]
    right = [right, right_near[0], across(right_near[0], "x"), right_near[1]]
    sorted_bases = sort_call(*bases, const["order"], const["columns"])
    prepared = base_call(left, right, *sorted_bases, const["unit"])
    second, *prepared = lax.optimization_barrier((second, *prepared))
    other = swap_core(second)
    keep, send = layer_call(
        place,
        second,
        other,
        left,
        right,
        prepared[0],
        const["pair"],
        const["pair_t"],
        fast_scales,
        const["window"],
        *prepared[1:],
    )
    backs = (keep.astype(F32) + swap_core(send).astype(F32)).astype(BF)
    backs = lax.all_to_all(
        backs.reshape(128, 8, 640), HALVES, split_axis=0, concat_axis=0, tiled=True
    ).reshape(2, 512, 640)
    folded = revert_call(adjoint, gains, h512, backs)
    folded = lax.all_to_all(
        folded.reshape(64, 8, 640), FSDP, split_axis=0, concat_axis=0, tiled=True
    )
    part = land_call(place, signs, const["half_t"], folded.reshape(512, 640))
    others = [
        lax.ppermute(part, ("zh", "co"), [(i, i ^ by) for i in range(4)]) for by in (3, 2, 1)
    ]
    return part + others[0] + others[1] + others[2]


def solution(mesh):
    split = Mesh(mesh.devices.reshape(2, 2, 4, 4, 4), AXES)
    group = ("zh", "co")
    in_specs = (
        P(group + FSDP, None),
        P(group + FSDP, None),
        P(None, FSDP),
        P(None, FSDP),
        P(FSDP, None),
        P(FSDP, None),
        P(None, FSDP, None, None),
        P(None, None, FSDP, None),
        P(None, FSDP, None),
        P(),
    )
    return jax.shard_map(
        on_device, mesh=split, in_specs=in_specs, out_specs=P(FSDP, None), check_vma=False
    )
```

```python
import functools

import jax
import jax.numpy as jnp
import numpy as np
from jax import lax
from jax.experimental import pallas as pl
from jax.experimental.pallas import tpu as pltpu
from jax.sharding import Mesh, PartitionSpec as P

D = 4096
FF = 10240
BF = jnp.bfloat16
F32 = jnp.float32
AXES = ("zh", "co", "y", "x", "zl")
FSDP = ("y", "x", "zl")
HALVES = ("zh", "y", "x", "zl")
VMEM_BYTES = 60 * 1024 * 1024


def sylvester(size):
    matrix = np.ones((1, 1), np.float32)
    while matrix.shape[0] < size:
        matrix = np.block([[matrix, matrix], [matrix, -matrix]])
    return matrix


@functools.cache
def tables():
    h128, h512 = sylvester(128), sylvester(512)
    half = np.stack([h128[par::2] for par in range(2)])
    pair = np.stack([np.concatenate([h128[:, par::2], h128[:, 1 - par :: 2]], 1) for par in range(2)])
    hidden = np.arange(160)
    place = (hidden % 5) * 32 + hidden // 5
    window = np.zeros((4, 256, 160), np.float32)
    for q in range(4):
        window[q, 32 * q + hidden, place] = 1
    order = np.zeros((160, 160), np.float32)
    order[place, hidden] = 1
    columns = np.zeros((512, 512), np.float32)
    q, r = np.divmod(np.arange(512), 128)
    columns[np.arange(512), r * 4 + q] = 1
    apart = np.zeros((32, 32), np.float32)
    row = np.arange(16)
    apart[row, (row // 4) * 8 + row % 4] = 1
    apart[16 + row, (row // 4) * 8 + 4 + row % 4] = 1
    cast = lambda value: np.ascontiguousarray(value).astype(BF)
    return dict(
        half=cast(half),
        half_t=cast(half.transpose(0, 2, 1)),
        pair=cast(pair),
        pair_t=cast(pair.transpose(0, 2, 1)),
        h512=cast(h512),
        window=cast(window),
        order=cast(order),
        columns=cast(columns),
        apart=cast(apart),
        unit=cast(np.eye(256)),
    )


def butterfly(items):
    step = 1
    while step < len(items):
        items = [
            items[i] + items[i ^ step] if not i & step else items[i ^ step] - items[i]
            for i in range(len(items))
        ]
        step *= 2
    return items


def dot(left, right):
    return jnp.dot(left, right, preferred_element_type=F32)


def dot_t(left, right):
    return lax.dot_general(left, right, (((1,), (1,)), ((), ())), preferred_element_type=F32)


def dot_l(left, right):
    return lax.dot_general(left, right, (((0,), (0,)), ((), ())), preferred_element_type=F32)


def params():
    return pltpu.CompilerParams(vmem_limit_bytes=VMEM_BYTES)


def lift_kernel(place, sub, signs, half, out, flips, parts, rows, sems):
    copies = []
    for a in range(8):
        block = pl.ds(128 * a, 128)
        copies.append(pltpu.make_async_copy(signs.at[place[0], block], flips.at[block], sems.at[a]))
        copies[-1].start()
    grid = half[place[1]]
    for a in range(8):
        row = sub[a : a + 1, :]
        high = row.astype(BF)
        low = (row - high.astype(F32)).astype(BF)
        scaled = jnp.concatenate([grid * high, grid * low], axis=1)
        copies[a].wait()
        flip = flips[128 * a : 128 * (a + 1), :].astype(F32).astype(BF)
        parts[a] = dot(scaled, jnp.concatenate([flip, flip], axis=0))
    for kt in range(5):
        tile = slice(128 * kt, 128 * (kt + 1))
        for part in range(4):
            at = slice(16 * part, 16 * (part + 1))
            mixed = butterfly([parts[a, at, tile] for a in range(8)])
            for b in range(8):
                rows[kt, pl.ds(128 * part + b, 16, stride=8), :] = mixed[b]
    for kt in range(5):
        out[:, 128 * kt : 128 * (kt + 1)] = (rows[kt] * (1.0 / 32.0)).astype(BF)


def lift_call(place, subspace, signs, half):
    whole = pl.BlockSpec(memory_space=pltpu.VMEM)
    away = pl.BlockSpec(memory_space=pl.ANY)
    return pl.pallas_call(
        lift_kernel,
        out_shape=jax.ShapeDtypeStruct((512, 640), BF),
        in_specs=[pl.BlockSpec(memory_space=pltpu.SMEM), whole, away, whole],
        out_specs=whole,
        scratch_shapes=[
            pltpu.VMEM((1024, 640), jnp.int32),
            pltpu.VMEM((8, 64, 640), F32),
            pltpu.VMEM((5, 512, 128), F32),
            pltpu.SemaphoreType.DMA((8,)),
        ],
        compiler_params=params(),
        name="lift",
    )(place, subspace, signs, half)


def middle_kernel(mixer, gains, h512, first, *rest):
    out = rest[-1]
    turned = dot(mixer[...], first[...]) * 0.125
    mixed = (gains[...].astype(F32) * turned).astype(BF)
    second = (dot(h512[...], mixed) * 512**-0.5).astype(BF)
    out[0] = second
    out[1] = second


def middle_call(mixer, gains, h512, first, after=()):
    whole = pl.BlockSpec(memory_space=pltpu.VMEM)
    away = pl.BlockSpec(memory_space=pl.ANY)
    return pl.pallas_call(
        middle_kernel,
        out_shape=jax.ShapeDtypeStruct((2, 512, 640), BF),
        in_specs=[whole] * 4 + [away] * len(after),
        out_specs=whole,
        compiler_params=params(),
        name="middle",
    )(mixer, gains, h512, first, *after)


def revert_kernel(mixer, gains, h512, backs, out):
    spread = (dot(h512[...], backs[0]) + dot(h512[...], backs[1])) * 512**-0.5
    spread = (gains[...].astype(F32) * spread).astype(BF)
    out[...] = (dot(mixer[...], spread) * 0.125).astype(BF)


def revert_call(mixer, gains, h512, backs):
    return pl.pallas_call(
        revert_kernel,
        out_shape=jax.ShapeDtypeStruct((512, 640), BF),
        compiler_params=params(),
        name="revert",
    )(mixer, gains, h512, backs)


def land_kernel(place, signs, half_t, folded, out, flips, rows, parts, sems):
    copies = []
    for a in range(8):
        block = pl.ds(128 * a, 128)
        copies.append(pltpu.make_async_copy(signs.at[place[0], block], flips.at[block], sems.at[a]))
        copies[-1].start()
    grid = half_t[place[1]]
    for kt in range(5):
        rows[kt] = folded[:, 128 * kt : 128 * (kt + 1)].astype(F32)
    for a in range(8):
        block = [rows[kt, pl.ds(a, 64, stride=8), :] for kt in range(5)]
        parts[a] = dot(grid, jnp.concatenate(block, axis=1).astype(BF))
    for copy in copies:
        copy.wait()
    ones = jnp.ones((8, 128), BF)
    for part in range(8):
        at = slice(16 * part, 16 * (part + 1))
        lanes = [None] * 8
        for kt in range(5):
            tile = slice(128 * kt, 128 * (kt + 1))
            mixed = butterfly([parts[a, at, tile] for a in range(8)])
            for b in range(8):
                start = 128 * b + 16 * part
                term = mixed[b] * flips[start : start + 16, tile].astype(F32)
                lanes[b] = term if lanes[b] is None else lanes[b] + term
        for b in range(8):
            parts[b, at, 0:128] = lanes[b]
    for b in range(8):
        full = parts[b, :, 0:128]
        high = full.astype(BF)
        rest = full - high.astype(F32)
        low = rest.astype(BF)
        last = (rest - low.astype(F32)).astype(BF)
        sums = dot_t(ones, high) + dot_t(ones, low) + dot_t(ones, last)
        out[b : b + 1, :] = sums[0:1, :] * (1.0 / 32.0)


def land_call(place, signs, half_t, folded):
    whole = pl.BlockSpec(memory_space=pltpu.VMEM)
    away = pl.BlockSpec(memory_space=pl.ANY)
    return pl.pallas_call(
        land_kernel,
        out_shape=jax.ShapeDtypeStruct((8, 128), F32),
        in_specs=[pl.BlockSpec(memory_space=pltpu.SMEM), away, whole, whole],
        out_specs=whole,
        scratch_shapes=[
            pltpu.VMEM((1024, 640), jnp.int32),
            pltpu.VMEM((5, 512, 128), F32),
            pltpu.VMEM((8, 128, 640), F32),
            pltpu.SemaphoreType.DMA((8,)),
        ],
        compiler_params=params(),
        name="land",
    )(place, signs, half_t, folded)


def sort_columns(item, columns, target):
    height = item.shape[0]
    stack = jnp.concatenate([item[:, 512 * g : 512 * (g + 1)] for g in range(8)], axis=0)
    stack = dot_t(stack, columns).astype(BF)
    for g in range(8):
        for q in range(4):
            at = 1024 * q + 128 * g
            target[:, at : at + 128] = stack[height * g : height * (g + 1), 128 * q : 128 * (q + 1)]


def part_kernel(a, b, c, d, order, columns, left, right):
    stack = jnp.concatenate([item[...].astype(F32) for item in (a, b, c, d)], axis=0).astype(BF)
    apart = dot(order[...], stack).astype(BF)
    sort_columns(apart[0:16, :], columns[...], left)
    right[...] = apart[16:32, :]


def part_call(slots, order, columns):
    return pl.pallas_call(
        part_kernel,
        out_shape=[jax.ShapeDtypeStruct((16, 4096), BF)] * 2,
        compiler_params=params(),
        name="part",
    )(*slots, order, columns)


def join_kernel(*refs):
    ins, outs = refs[:8], refs[8:10]
    for i in range(8):
        outs[i // 4][16 * (i % 4) : 16 * (i % 4) + 16, :] = ins[i][...]


def join_call(left, right):
    return pl.pallas_call(
        join_kernel,
        out_shape=[jax.ShapeDtypeStruct((64, 4096), BF)] * 2,
        compiler_params=params(),
        name="join",
    )(*left, *right)


def sort_kernel(gate_base, up_base, out_base, order, columns, gate, up, out):
    for base, target in ((gate_base, gate), (up_base, up)):
        ordered = dot(order[...], base[...]).astype(BF)
        for g in range(8):
            turned = dot_t(columns[...], ordered[:, 512 * g : 512 * (g + 1)]).astype(BF)
            for q in range(4):
                at = 1024 * q + 128 * g
                target[at : at + 128, :] = turned[128 * q : 128 * (q + 1), :]
    out[...] = jnp.transpose(dot(order[...], out_base[...])).astype(BF)


def sort_call(*args):
    return pl.pallas_call(
        sort_kernel,
        out_shape=[jax.ShapeDtypeStruct((4096, 160), BF)] * 3,
        compiler_params=params(),
        name="sort",
    )(*args)


def collect(left, right, x, dy, sems):
    copies = [pltpu.make_async_copy(left[i], x.at[pl.ds(64 * i, 64)], sems.at[i]) for i in range(4)]
    late = [
        pltpu.make_async_copy(
            right[i].at[pl.ds(16 * j, 16)], dy.at[pl.ds(64 * j + 16 * i, 16)], sems.at[4 + 4 * i + j]
        )
        for i in range(4)
        for j in range(4)
    ]
    for copy in copies + late:
        copy.start()
    return copies, late


def base_kernel(*refs):
    left, right = refs[0:4], refs[4:8]
    bases, unit = refs[8:11], refs[11]
    x_rows_far, gate, up, grad = refs[12:16]
    x, dy, near, x_rows, sems, piece_sems = refs[16:22]
    loads = [pltpu.make_async_copy(bases[i], near.at[i], sems.at[i]) for i in range(3)]
    loads[0].start()
    first, late = collect(left, right, x, dy, piece_sems)
    for load in loads[1:]:
        load.start()
    for copy in first:
        copy.wait()
    loads[0].wait()
    gate[...] = dot(x[...], near[0])
    leaves = []
    for part in range(4):
        for g in range(4 * part, 4 * (part + 1)):
            at = slice(256 * g, 256 * (g + 1))
            x_rows[at, :] = dot_t(unit[...], x[:, at]).astype(BF)
        rows = pl.ds(1024 * part, 1024)
        leaves.append(
            pltpu.make_async_copy(x_rows.at[rows], x_rows_far.at[rows], sems.at[3 + part])
        )
        leaves[-1].start()
    loads[1].wait()
    up[...] = dot(x[...], near[1])
    for copy in late:
        copy.wait()
    loads[2].wait()
    grad[...] = dot(dy[...], near[2])
    for leave in leaves:
        leave.wait()


COST = 2 * 10**10


def base_call(left, right, gate_base, up_base, out_base, unit):
    whole = pl.BlockSpec(memory_space=pltpu.VMEM)
    away = pl.BlockSpec(memory_space=pl.ANY)
    return pl.pallas_call(
        base_kernel,
        out_shape=[jax.ShapeDtypeStruct((4096, 256), BF)]
        + [jax.ShapeDtypeStruct((256, 160), F32)] * 3,
        in_specs=[away] * 11 + [whole],
        out_specs=[away] + [whole] * 3,
        scratch_shapes=[
            pltpu.VMEM((256, 4096), BF),
            pltpu.VMEM((256, 4096), BF),
            pltpu.VMEM((3, 4096, 160), BF),
            pltpu.VMEM((4096, 256), BF),
            pltpu.SemaphoreType.DMA((7,)),
            pltpu.SemaphoreType.DMA((20,)),
        ],
        compiler_params=params(),
        cost_estimate=pl.CostEstimate(flops=COST, bytes_accessed=10**6, transcendentals=0),
        name="base",
    )(*left, *right, gate_base, up_base, out_base, unit)


def layer_kernel(
    place,
    own_far,
    other_far,
    l0,
    l1,
    l2,
    l3,
    r0,
    r1,
    r2,
    r3,
    x_rows_far,
    pair,
    pair_t,
    scales,
    window,
    gate_part,
    up_part,
    grad_part,
    keep_far,
    send_far,
    own,
    other,
    x_cols,
    x_rows,
    dy,
    near,
    tall,
    e0,
    w1,
    keep,
    send,
    sems,
    piece_sems,
):
    mine = place[1]
    count = [0]
    waits = {}

    def bring(key, source, target):
        copy = pltpu.make_async_copy(source, target, sems.at[count[0]])
        count[0] += 1
        copy.start()
        waits[key] = copy

    for m in range(2):
        bring(("own", m), own_far.at[m], own.at[m])
        bring(("other", m), other_far.at[m], other.at[m])
    first, late = collect((l0, l1, l2, l3), (r0, r1, r2, r3), x_cols, dy, piece_sems)
    bring("x_rows", x_rows_far, x_rows)

    factors = ((D**-0.5) * (128**-0.5), (FF**-0.5) * (128**-0.5))
    tiles = [slice(128 * kt, 128 * (kt + 1)) for kt in range(5)]
    grid, grid_t = pair[mine], pair_t[mine]

    def widen(m, put):
        waits[("own", m)].wait()
        waits[("other", m)].wait()
        for kt in range(5):
            near[0, kt] = own[m, :, tiles[kt]].astype(F32)
            near[1, kt] = other[m, :, tiles[kt]].astype(F32)
        for b in range(8):
            block = jnp.concatenate(
                [
                    jnp.concatenate(
                        [near[side, kt, pl.ds(b, 64, stride=8), :] for kt in range(5)], axis=1
                    )
                    for side in range(2)
                ],
                axis=0,
            ).astype(BF)
            put(b, dot(grid, block) * (scales[m, b : b + 1, :] * factors[m]))

    def put0(b, wide):
        e0[128 * b : 128 * (b + 1), :] = wide.astype(BF)

    def put1(b, wide):
        for kt in range(5):
            tall[kt, 128 * b : 128 * (b + 1), :] = wide[:, tiles[kt]]

    widen(0, put0)
    for copy in first + late + [waits["x_rows"]]:
        copy.wait()
    widen(1, put1)
    for w in range(32):
        for kt in range(5):
            v, jt = divmod(5 * w + kt, 32)
            w1[32 * v : 32 * (v + 1), 128 * jt : 128 * (jt + 1)] = tall[
                kt, pl.ds(w, 32, stride=32), :
            ].astype(BF)
    gate = gate_part[...]
    for q in range(4):
        part = dot(x_cols[:, 1024 * q : 1024 * (q + 1)], e0[:, 128 * q : 128 * q + 256])
        high = part.astype(BF)
        low = (part - high.astype(F32)).astype(BF)
        gate = gate + dot(high, window[q]) + dot(low, window[q])
    up = up_part[...]
    grad = grad_part[...] + dot_t(dy[...], w1[...])
    argument = 0.7978845608028654 * (gate + 0.044715 * gate * gate * gate)
    tangent = jnp.tanh(argument)
    half = 0.5 * (1.0 + tangent)
    hidden = (gate * half * up).astype(BF)
    slope = half + 0.5 * gate * (1.0 - tangent * tangent) * 0.7978845608028654 * (
        1.0 + 0.134145 * gate * gate
    )
    gate_grad = (grad * up * slope).astype(BF)
    out_grad = dot_l(hidden, dy[...])
    for w in range(32):
        for kt in range(5):
            v, jt = divmod(5 * w + kt, 32)
            tall[kt, pl.ds(w, 32, stride=32), :] = out_grad[
                32 * v : 32 * (v + 1), 128 * jt : 128 * (jt + 1)
            ]

    def leave(m, get):
        for b in range(8):
            back = dot(grid_t, (get(b) * (scales[m, b : b + 1, :] * factors[m])).astype(BF))
            for kt in range(5):
                near[0, kt, pl.ds(b, 64, stride=8), :] = back[0:64, tiles[kt]]
                near[1, kt, pl.ds(b, 64, stride=8), :] = back[64:128, tiles[kt]]
        for kt in range(5):
            send[m, :, tiles[kt]] = near[1, kt].astype(BF)
            keep[m, :, tiles[kt]] = near[0, kt].astype(BF)
        bring(("send", m), send.at[m], send_far.at[m])
        bring(("keep", m), keep.at[m], keep_far.at[m])

    def rows_of(b):
        return jnp.concatenate([tall[kt, 128 * b : 128 * (b + 1), :] for kt in range(5)], axis=1)

    leave(1, rows_of)
    windows = [dot_t(gate_grad, window[q]).astype(BF) for q in range(4)]

    for q in range(4):
        part = dot(x_rows[1024 * q : 1024 * (q + 1), :], windows[q])
        tall[q] = part[:, 0:128] + tall[q] if q else part[:, 0:128]
        tall[q + 1] = part[:, 128:256]

    leave(0, rows_of)
    for m in range(2):
        for side in ("send", "keep"):
            waits[(side, m)].wait()


def layer_call(place, own, other, left, right, x_rows, *args):
    whole = pl.BlockSpec(memory_space=pltpu.VMEM)
    away = pl.BlockSpec(memory_space=pl.ANY)
    return pl.pallas_call(
        layer_kernel,
        out_shape=[jax.ShapeDtypeStruct((2, 512, 640), BF)] * 2,
        in_specs=[pl.BlockSpec(memory_space=pltpu.SMEM)] + [away] * 11 + [whole] * len(args),
        out_specs=[away] * 2,
        scratch_shapes=[
            pltpu.VMEM((2, 512, 640), BF),
            pltpu.VMEM((2, 512, 640), BF),
            pltpu.VMEM((256, 4096), BF),
            pltpu.VMEM((4096, 256), BF),
            pltpu.VMEM((256, 4096), BF),
            pltpu.VMEM((2, 5, 512, 128), F32),
            pltpu.VMEM((5, 1024, 128), F32),
            pltpu.VMEM((1024, 640), BF),
            pltpu.VMEM((160, 4096), BF),
            pltpu.VMEM((2, 512, 640), BF),
            pltpu.VMEM((2, 512, 640), BF),
            pltpu.SemaphoreType.DMA((9,)),
            pltpu.SemaphoreType.DMA((20,)),
        ],
        compiler_params=params(),
        name="layer",
    )(place, own, other, *left, *right, x_rows, *args)


def shifted(item, axis):
    return [item] + [
        lax.ppermute(item, axis, [(i, (i + by) % 4) for i in range(4)]) for by in (1, 2, 3)
    ]


def hop(item, axis, by):
    pairs = [
        (4 * core + i, 4 * core + (i + (by if core == 0 else -by)) % 4)
        for core in range(2)
        for i in range(4)
    ]
    return lax.ppermute(item, ("co", axis), pairs)


def near_two(item, axis):
    return [hop(item, axis, by) for by in (1, 3)]


def across(back, axis):
    return hop(back, axis, 1)


def swap_core(item):
    return lax.ppermute(item, "co", [(0, 1), (1, 0)])


def mixers(order):
    block = jnp.arange(512, dtype=jnp.int32)

    def build(left, right):
        both = (left >> 3) & (right >> 3)
        both = both ^ (both >> 4)
        both = both ^ (both >> 2)
        both = both ^ (both >> 1)
        sign = 1 - 2 * (both & 1)
        return jnp.where((left & 7) == (right & 7), sign, 0).astype(BF)

    return build(order[:, None], block[None, :]), build(block[:, None], order[None, :])


def on_device(
    tokens,
    cotangent,
    gate_base,
    up_base,
    out_base,
    subspace,
    sign_flips,
    fast_gains,
    fast_scales,
    block_orders,
):
    const = tables()
    which, core = lax.axis_index("zh"), lax.axis_index("co")
    place = jnp.stack([which, core]).astype(jnp.int32)
    signs = sign_flips.reshape(2, 1024, 640)

    both, place = lax.optimization_barrier((jnp.concatenate([tokens, cotangent], axis=0), place))
    slots = shifted(both, "zl")
    first = lift_call(place, subspace, signs, const["half"])
    left, right = part_call(slots, const["apart"], const["columns"])
    first, left, right = lax.optimization_barrier((first, left, right))
    left_near, right_near = near_two(left, "x"), near_two(right, "y")
    order = lax.dynamic_index_in_dim(block_orders, which, 0, keepdims=False)
    forward, adjoint = mixers(order)
    gains = lax.dynamic_slice(fast_gains, (which, 0, core, 0), (1, 512, 1, 640)).reshape(512, 640)
    left_near, right_near, forward, adjoint, gains = lax.optimization_barrier(
        (left_near, right_near, forward, adjoint, gains)
    )
    left, right = join_call(
        [left, left_near[0], across(left_near[0], "x"), left_near[1]],
        [right, right_near[0], across(right_near[0], "y"), right_near[1]],
    )
    stage = (left, right)
    left_near, right_near = near_two(left, "y"), near_two(right, "x")
    first = lax.all_to_all(first.reshape(64, 8, 640), FSDP, split_axis=0, concat_axis=0, tiled=True)

    h512 = const["h512"]
    second = middle_call(forward, gains, h512, first.reshape(512, 640), stage)
    _, left_near, right_near, bases = lax.optimization_barrier(
        (second, left_near, right_near, (gate_base.T, up_base.T, out_base))
    )
    second = lax.all_to_all(
        second.reshape(128, 8, 640), HALVES, split_axis=0, concat_axis=0, tiled=True
    ).reshape(2, 512, 640)
    left = [left, left_near[0], across(left_near[0], "y"), left_near[1]]
    right = [right, right_near[0], across(right_near[0], "x"), right_near[1]]
    sorted_bases = sort_call(*bases, const["order"], const["columns"])
    prepared = base_call(left, right, *sorted_bases, const["unit"])
    second, *prepared = lax.optimization_barrier((second, *prepared))
    other = swap_core(second)
    keep, send = layer_call(
        place,
        second,
        other,
        left,
        right,
        prepared[0],
        const["pair"],
        const["pair_t"],
        fast_scales,
        const["window"],
        *prepared[1:],
    )
    backs = (keep.astype(F32) + swap_core(send).astype(F32)).astype(BF)
    backs = lax.all_to_all(
        backs.reshape(128, 8, 640), HALVES, split_axis=0, concat_axis=0, tiled=True
    ).reshape(2, 512, 640)
    folded = revert_call(adjoint, gains, h512, backs)
    folded = lax.all_to_all(
        folded.reshape(64, 8, 640), FSDP, split_axis=0, concat_axis=0, tiled=True
    )
    part = land_call(place, signs, const["half_t"], folded.reshape(512, 640))
    part = part + swap_core(part)
    return part + lax.ppermute(part, "zh", [(0, 1), (1, 0)])


def solution(mesh):
    split = Mesh(mesh.devices.reshape(2, 2, 4, 4, 4), AXES)
    group = ("zh", "co")
    in_specs = (
        P(group + FSDP, None),
        P(group + FSDP, None),
        P(None, FSDP),
        P(None, FSDP),
        P(FSDP, None),
        P(FSDP, None),
        P(None, FSDP, None, None),
        P(None, None, FSDP, None),
        P(None, FSDP, None),
        P(),
    )
    return jax.shard_map(
        on_device, mesh=split, in_specs=in_specs, out_specs=P(FSDP, None), check_vma=False
    )
```

```python
import functools

import jax
import jax.numpy as jnp
import numpy as np
from jax import lax
from jax.experimental import pallas as pl
from jax.experimental.pallas import tpu as pltpu
from jax.sharding import Mesh, PartitionSpec as P

D = 4096
FF = 10240
BF = jnp.bfloat16
F32 = jnp.float32
AXES = ("zh", "co", "y", "x", "zl")
FSDP = ("y", "x", "zl")
HALVES = ("zh", "y", "x", "zl")
VMEM_BYTES = 60 * 1024 * 1024


def sylvester(size):
    matrix = np.ones((1, 1), np.float32)
    while matrix.shape[0] < size:
        matrix = np.block([[matrix, matrix], [matrix, -matrix]])
    return matrix


@functools.cache
def tables():
    h128, h512 = sylvester(128), sylvester(512)
    half = np.stack([h128[par::2] for par in range(2)])
    pair = np.stack([np.concatenate([h128[:, par::2], h128[:, 1 - par :: 2]], 1) for par in range(2)])
    hidden = np.arange(160)
    place = (hidden % 5) * 32 + hidden // 5
    window = np.zeros((4, 256, 160), np.float32)
    for q in range(4):
        window[q, 32 * q + hidden, place] = 1
    order = np.zeros((160, 160), np.float32)
    order[place, hidden] = 1
    columns = np.zeros((512, 512), np.float32)
    q, r = np.divmod(np.arange(512), 128)
    columns[np.arange(512), r * 4 + q] = 1
    apart = np.zeros((32, 32), np.float32)
    row = np.arange(16)
    apart[row, (row // 4) * 8 + row % 4] = 1
    apart[16 + row, (row // 4) * 8 + 4 + row % 4] = 1
    cast = lambda value: np.ascontiguousarray(value).astype(BF)
    return dict(
        half=cast(half),
        half_t=cast(half.transpose(0, 2, 1)),
        pair=cast(pair),
        pair_t=cast(pair.transpose(0, 2, 1)),
        h512=cast(h512),
        window=cast(window),
        order=cast(order),
        columns=cast(columns),
        apart=cast(apart),
        unit=cast(np.eye(256)),
    )


def butterfly(items):
    step = 1
    while step < len(items):
        items = [
            items[i] + items[i ^ step] if not i & step else items[i ^ step] - items[i]
            for i in range(len(items))
        ]
        step *= 2
    return items


def dot(left, right):
    return jnp.dot(left, right, preferred_element_type=F32)


def dot_t(left, right):
    return lax.dot_general(left, right, (((1,), (1,)), ((), ())), preferred_element_type=F32)


def dot_l(left, right):
    return lax.dot_general(left, right, (((0,), (0,)), ((), ())), preferred_element_type=F32)


def params():
    return pltpu.CompilerParams(vmem_limit_bytes=VMEM_BYTES)


def lift_kernel(place, sub, signs, half, out, flips, parts, rows, sems):
    copies = []
    for a in range(8):
        block = pl.ds(128 * a, 128)
        copies.append(pltpu.make_async_copy(signs.at[place[0], block], flips.at[block], sems.at[a]))
        copies[-1].start()
    grid = half[place[1]]
    for a in range(8):
        row = sub[a : a + 1, :]
        high = row.astype(BF)
        low = (row - high.astype(F32)).astype(BF)
        scaled = jnp.concatenate([grid * high, grid * low], axis=1)
        copies[a].wait()
        flip = flips[128 * a : 128 * (a + 1), :].astype(F32).astype(BF)
        parts[a] = dot(scaled, jnp.concatenate([flip, flip], axis=0))
    for kt in range(5):
        tile = slice(128 * kt, 128 * (kt + 1))
        for part in range(4):
            at = slice(16 * part, 16 * (part + 1))
            mixed = butterfly([parts[a, at, tile] for a in range(8)])
            for b in range(8):
                rows[kt, pl.ds(128 * part + b, 16, stride=8), :] = mixed[b]
    for kt in range(5):
        out[:, 128 * kt : 128 * (kt + 1)] = (rows[kt] * (1.0 / 32.0)).astype(BF)


def lift_call(place, subspace, signs, half):
    whole = pl.BlockSpec(memory_space=pltpu.VMEM)
    away = pl.BlockSpec(memory_space=pl.ANY)
    return pl.pallas_call(
        lift_kernel,
        out_shape=jax.ShapeDtypeStruct((512, 640), BF),
        in_specs=[pl.BlockSpec(memory_space=pltpu.SMEM), whole, away, whole],
        out_specs=whole,
        scratch_shapes=[
            pltpu.VMEM((1024, 640), jnp.int32),
            pltpu.VMEM((8, 64, 640), F32),
            pltpu.VMEM((5, 512, 128), F32),
            pltpu.SemaphoreType.DMA((8,)),
        ],
        compiler_params=params(),
        name="lift",
    )(place, subspace, signs, half)


def fetch(sources, targets, sems):
    copies = [
        pltpu.make_async_copy(source, target, sems.at[i])
        for i, (source, target) in enumerate(zip(sources, targets))
    ]
    for copy in copies:
        copy.start()
    return copies


def middle_kernel(first_far, mixer_far, gains_far, h512_far, *rest):
    out_far = rest[-7]
    first, mixer, gains, h512, out, sems = rest[-6:]
    copies = fetch((first_far, mixer_far, gains_far, h512_far), (first, mixer, gains, h512), sems)
    copies[0].wait()
    copies[1].wait()
    turned = dot(mixer[...], first[...]) * 0.125
    copies[2].wait()
    mixed = (gains[...].astype(F32) * turned).astype(BF)
    copies[3].wait()
    leaves = []
    for part in range(2):
        rows = pl.ds(256 * part, 256)
        out[256 * part : 256 * (part + 1), :] = (
            dot(h512[256 * part : 256 * (part + 1), :], mixed) * 512**-0.5
        ).astype(BF)
        for half in range(2):
            leaves.append(
                pltpu.make_async_copy(out.at[rows], out_far.at[half, rows], sems.at[4 + len(leaves)])
            )
            leaves[-1].start()
    for leave in leaves:
        leave.wait()


def middle_call(mixer, gains, h512, first, after=()):
    away = pl.BlockSpec(memory_space=pl.ANY)
    return pl.pallas_call(
        middle_kernel,
        out_shape=jax.ShapeDtypeStruct((2, 512, 640), BF),
        in_specs=[away] * (4 + len(after)),
        out_specs=away,
        scratch_shapes=[
            pltpu.VMEM((512, 640), BF),
            pltpu.VMEM((512, 512), BF),
            pltpu.VMEM((512, 640), BF),
            pltpu.VMEM((512, 512), BF),
            pltpu.VMEM((512, 640), BF),
            pltpu.SemaphoreType.DMA((8,)),
        ],
        compiler_params=params(),
        name="middle",
    )(first, mixer, gains, h512, *after)


def revert_kernel(
    backs_far, h512_far, gains_far, mixer_far, out_far, backs, h512, gains, mixer, out, sems
):
    copies = fetch(
        (h512_far, backs_far.at[0], backs_far.at[1], gains_far, mixer_far),
        (h512, backs.at[0], backs.at[1], gains, mixer),
        sems,
    )
    copies[0].wait()
    copies[1].wait()
    spread = dot(h512[...], backs[0])
    copies[2].wait()
    spread = (spread + dot(h512[...], backs[1])) * 512**-0.5
    copies[3].wait()
    spread = (gains[...].astype(F32) * spread).astype(BF)
    copies[4].wait()
    leaves = []
    for part in range(2):
        rows = pl.ds(256 * part, 256)
        out[256 * part : 256 * (part + 1), :] = (
            dot(mixer[256 * part : 256 * (part + 1), :], spread) * 0.125
        ).astype(BF)
        leaves.append(pltpu.make_async_copy(out.at[rows], out_far.at[rows], sems.at[5 + part]))
        leaves[-1].start()
    for leave in leaves:
        leave.wait()


def revert_call(mixer, gains, h512, backs):
    away = pl.BlockSpec(memory_space=pl.ANY)
    return pl.pallas_call(
        revert_kernel,
        out_shape=jax.ShapeDtypeStruct((512, 640), BF),
        in_specs=[away] * 4,
        out_specs=away,
        scratch_shapes=[
            pltpu.VMEM((2, 512, 640), BF),
            pltpu.VMEM((512, 512), BF),
            pltpu.VMEM((512, 640), BF),
            pltpu.VMEM((512, 512), BF),
            pltpu.VMEM((512, 640), BF),
            pltpu.SemaphoreType.DMA((7,)),
        ],
        compiler_params=params(),
        name="revert",
    )(backs, h512, gains, mixer)


def land_kernel(place, signs, half_t, folded, out, flips, rows, parts, sems):
    copies = []
    for a in range(8):
        block = pl.ds(128 * a, 128)
        copies.append(pltpu.make_async_copy(signs.at[place[0], block], flips.at[block], sems.at[a]))
        copies[-1].start()
    grid = half_t[place[1]]
    for kt in range(5):
        rows[kt] = folded[:, 128 * kt : 128 * (kt + 1)].astype(F32)
    for a in range(8):
        block = [rows[kt, pl.ds(a, 64, stride=8), :] for kt in range(5)]
        parts[a] = dot(grid, jnp.concatenate(block, axis=1).astype(BF))
    for copy in copies:
        copy.wait()
    ones = jnp.ones((8, 128), BF)
    for part in range(8):
        at = slice(16 * part, 16 * (part + 1))
        lanes = [None] * 8
        for kt in range(5):
            tile = slice(128 * kt, 128 * (kt + 1))
            mixed = butterfly([parts[a, at, tile] for a in range(8)])
            for b in range(8):
                start = 128 * b + 16 * part
                term = mixed[b] * flips[start : start + 16, tile].astype(F32)
                lanes[b] = term if lanes[b] is None else lanes[b] + term
        for b in range(8):
            parts[b, at, 0:128] = lanes[b]
    for b in range(8):
        full = parts[b, :, 0:128]
        high = full.astype(BF)
        rest = full - high.astype(F32)
        low = rest.astype(BF)
        last = (rest - low.astype(F32)).astype(BF)
        sums = dot_t(ones, high) + dot_t(ones, low) + dot_t(ones, last)
        out[b : b + 1, :] = sums[0:1, :] * (1.0 / 32.0)


def land_call(place, signs, half_t, folded):
    whole = pl.BlockSpec(memory_space=pltpu.VMEM)
    away = pl.BlockSpec(memory_space=pl.ANY)
    return pl.pallas_call(
        land_kernel,
        out_shape=jax.ShapeDtypeStruct((8, 128), F32),
        in_specs=[pl.BlockSpec(memory_space=pltpu.SMEM), away, whole, whole],
        out_specs=whole,
        scratch_shapes=[
            pltpu.VMEM((1024, 640), jnp.int32),
            pltpu.VMEM((5, 512, 128), F32),
            pltpu.VMEM((8, 128, 640), F32),
            pltpu.SemaphoreType.DMA((8,)),
        ],
        compiler_params=params(),
        name="land",
    )(place, signs, half_t, folded)


def sort_columns(item, columns, target):
    height = item.shape[0]
    stack = jnp.concatenate([item[:, 512 * g : 512 * (g + 1)] for g in range(8)], axis=0)
    stack = dot_t(stack, columns).astype(BF)
    for g in range(8):
        for q in range(4):
            at = 1024 * q + 128 * g
            target[:, at : at + 128] = stack[height * g : height * (g + 1), 128 * q : 128 * (q + 1)]


def part_kernel(a, b, c, d, order, columns, left, right):
    stack = jnp.concatenate([item[...].astype(F32) for item in (a, b, c, d)], axis=0).astype(BF)
    apart = dot(order[...], stack).astype(BF)
    sort_columns(apart[0:16, :], columns[...], left)
    right[...] = apart[16:32, :]


def part_call(slots, order, columns):
    return pl.pallas_call(
        part_kernel,
        out_shape=[jax.ShapeDtypeStruct((16, 4096), BF)] * 2,
        compiler_params=params(),
        name="part",
    )(*slots, order, columns)


def join_kernel(*refs):
    ins, outs = refs[:8], refs[8:10]
    for i in range(8):
        outs[i // 4][16 * (i % 4) : 16 * (i % 4) + 16, :] = ins[i][...]


JOIN_COST = 10**10


def join_call(left, right):
    return pl.pallas_call(
        join_kernel,
        out_shape=[jax.ShapeDtypeStruct((64, 4096), BF)] * 2,
        compiler_params=params(),
        cost_estimate=pl.CostEstimate(flops=JOIN_COST, bytes_accessed=10**6, transcendentals=0),
        name="join",
    )(*left, *right)


def sort_kernel(gate_base, up_base, out_base, order, columns, gate, up, out):
    for base, target in ((gate_base, gate), (up_base, up)):
        ordered = dot(order[...], base[...]).astype(BF)
        for g in range(8):
            turned = dot_t(columns[...], ordered[:, 512 * g : 512 * (g + 1)]).astype(BF)
            for q in range(4):
                at = 1024 * q + 128 * g
                target[at : at + 128, :] = turned[128 * q : 128 * (q + 1), :]
    out[...] = jnp.transpose(dot(order[...], out_base[...])).astype(BF)


def sort_call(*args):
    return pl.pallas_call(
        sort_kernel,
        out_shape=[jax.ShapeDtypeStruct((4096, 160), BF)] * 3,
        compiler_params=params(),
        name="sort",
    )(*args)


def collect(left, right, x, dy, sems):
    copies = [pltpu.make_async_copy(left[i], x.at[pl.ds(64 * i, 64)], sems.at[i]) for i in range(4)]
    late = [
        pltpu.make_async_copy(
            right[i].at[pl.ds(16 * j, 16)], dy.at[pl.ds(64 * j + 16 * i, 16)], sems.at[4 + 4 * i + j]
        )
        for i in range(4)
        for j in range(4)
    ]
    for copy in copies + late:
        copy.start()
    return copies, late


def base_kernel(*refs):
    left, right = refs[0:4], refs[4:8]
    bases, unit = refs[8:11], refs[11]
    x_rows_far, gate, up, grad = refs[12:16]
    x, dy, near, x_rows, sems, piece_sems = refs[16:22]
    loads = [pltpu.make_async_copy(bases[i], near.at[i], sems.at[i]) for i in range(3)]
    loads[0].start()
    first, late = collect(left, right, x, dy, piece_sems)
    for load in loads[1:]:
        load.start()
    for copy in first:
        copy.wait()
    loads[0].wait()
    gate[...] = dot(x[...], near[0])
    leaves = []
    for part in range(4):
        for g in range(4 * part, 4 * (part + 1)):
            at = slice(256 * g, 256 * (g + 1))
            x_rows[at, :] = dot_t(unit[...], x[:, at]).astype(BF)
        rows = pl.ds(1024 * part, 1024)
        leaves.append(
            pltpu.make_async_copy(x_rows.at[rows], x_rows_far.at[rows], sems.at[3 + part])
        )
        leaves[-1].start()
    loads[1].wait()
    up[...] = dot(x[...], near[1])
    for copy in late:
        copy.wait()
    loads[2].wait()
    grad[...] = dot(dy[...], near[2])
    for leave in leaves:
        leave.wait()


COST = 2 * 10**10


def base_call(left, right, gate_base, up_base, out_base, unit):
    whole = pl.BlockSpec(memory_space=pltpu.VMEM)
    away = pl.BlockSpec(memory_space=pl.ANY)
    return pl.pallas_call(
        base_kernel,
        out_shape=[jax.ShapeDtypeStruct((4096, 256), BF)]
        + [jax.ShapeDtypeStruct((256, 160), F32)] * 3,
        in_specs=[away] * 11 + [whole],
        out_specs=[away] + [whole] * 3,
        scratch_shapes=[
            pltpu.VMEM((256, 4096), BF),
            pltpu.VMEM((256, 4096), BF),
            pltpu.VMEM((3, 4096, 160), BF),
            pltpu.VMEM((4096, 256), BF),
            pltpu.SemaphoreType.DMA((7,)),
            pltpu.SemaphoreType.DMA((20,)),
        ],
        compiler_params=params(),
        cost_estimate=pl.CostEstimate(flops=COST, bytes_accessed=10**6, transcendentals=0),
        name="base",
    )(*left, *right, gate_base, up_base, out_base, unit)


def layer_kernel(
    place,
    own_far,
    other_far,
    l0,
    l1,
    l2,
    l3,
    r0,
    r1,
    r2,
    r3,
    x_rows_far,
    pair,
    pair_t,
    scales,
    window,
    gate_part,
    up_part,
    grad_part,
    keep_far,
    send_far,
    own,
    other,
    x_cols,
    x_rows,
    dy,
    near,
    tall,
    e0,
    w1,
    keep,
    send,
    sems,
    piece_sems,
):
    mine = place[1]
    count = [0]
    waits = {}

    def bring(key, source, target):
        copy = pltpu.make_async_copy(source, target, sems.at[count[0]])
        count[0] += 1
        copy.start()
        waits[key] = copy

    for m in range(2):
        bring(("own", m), own_far.at[m], own.at[m])
        bring(("other", m), other_far.at[m], other.at[m])
    first, late = collect((l0, l1, l2, l3), (r0, r1, r2, r3), x_cols, dy, piece_sems)
    bring("x_rows", x_rows_far, x_rows)

    factors = ((D**-0.5) * (128**-0.5), (FF**-0.5) * (128**-0.5))
    tiles = [slice(128 * kt, 128 * (kt + 1)) for kt in range(5)]
    grid, grid_t = pair[mine], pair_t[mine]

    def widen(m, put):
        waits[("own", m)].wait()
        waits[("other", m)].wait()
        for kt in range(5):
            near[0, kt] = own[m, :, tiles[kt]].astype(F32)
            near[1, kt] = other[m, :, tiles[kt]].astype(F32)
        for b in range(8):
            block = jnp.concatenate(
                [
                    jnp.concatenate(
                        [near[side, kt, pl.ds(b, 64, stride=8), :] for kt in range(5)], axis=1
                    )
                    for side in range(2)
                ],
                axis=0,
            ).astype(BF)
            put(b, dot(grid, block) * (scales[m, b : b + 1, :] * factors[m]))

    def put0(b, wide):
        e0[128 * b : 128 * (b + 1), :] = wide.astype(BF)

    def put1(b, wide):
        for kt in range(5):
            tall[kt, 128 * b : 128 * (b + 1), :] = wide[:, tiles[kt]]

    widen(0, put0)
    for copy in first + late + [waits["x_rows"]]:
        copy.wait()
    widen(1, put1)
    for w in range(32):
        for kt in range(5):
            v, jt = divmod(5 * w + kt, 32)
            w1[32 * v : 32 * (v + 1), 128 * jt : 128 * (jt + 1)] = tall[
                kt, pl.ds(w, 32, stride=32), :
            ].astype(BF)
    gate = gate_part[...]
    for q in range(4):
        part = dot(x_cols[:, 1024 * q : 1024 * (q + 1)], e0[:, 128 * q : 128 * q + 256])
        high = part.astype(BF)
        low = (part - high.astype(F32)).astype(BF)
        gate = gate + dot(high, window[q]) + dot(low, window[q])
    up = up_part[...]
    grad = grad_part[...] + dot_t(dy[...], w1[...])
    argument = 0.7978845608028654 * (gate + 0.044715 * gate * gate * gate)
    tangent = jnp.tanh(argument)
    half = 0.5 * (1.0 + tangent)
    hidden = (gate * half * up).astype(BF)
    slope = half + 0.5 * gate * (1.0 - tangent * tangent) * 0.7978845608028654 * (
        1.0 + 0.134145 * gate * gate
    )
    gate_grad = (grad * up * slope).astype(BF)
    out_grad = dot_l(hidden, dy[...])
    for w in range(32):
        for kt in range(5):
            v, jt = divmod(5 * w + kt, 32)
            tall[kt, pl.ds(w, 32, stride=32), :] = out_grad[
                32 * v : 32 * (v + 1), 128 * jt : 128 * (jt + 1)
            ]

    def leave(m, get):
        for b in range(8):
            back = dot(grid_t, (get(b) * (scales[m, b : b + 1, :] * factors[m])).astype(BF))
            for kt in range(5):
                near[0, kt, pl.ds(b, 64, stride=8), :] = back[0:64, tiles[kt]]
                near[1, kt, pl.ds(b, 64, stride=8), :] = back[64:128, tiles[kt]]
        for kt in range(5):
            send[m, :, tiles[kt]] = near[1, kt].astype(BF)
            keep[m, :, tiles[kt]] = near[0, kt].astype(BF)
        bring(("send", m), send.at[m], send_far.at[m])
        bring(("keep", m), keep.at[m], keep_far.at[m])

    def rows_of(b):
        return jnp.concatenate([tall[kt, 128 * b : 128 * (b + 1), :] for kt in range(5)], axis=1)

    leave(1, rows_of)
    windows = [dot_t(gate_grad, window[q]).astype(BF) for q in range(4)]

    for q in range(4):
        part = dot(x_rows[1024 * q : 1024 * (q + 1), :], windows[q])
        tall[q] = part[:, 0:128] + tall[q] if q else part[:, 0:128]
        tall[q + 1] = part[:, 128:256]

    leave(0, rows_of)
    for m in range(2):
        for side in ("send", "keep"):
            waits[(side, m)].wait()


def layer_call(place, own, other, left, right, x_rows, *args):
    whole = pl.BlockSpec(memory_space=pltpu.VMEM)
    away = pl.BlockSpec(memory_space=pl.ANY)
    return pl.pallas_call(
        layer_kernel,
        out_shape=[jax.ShapeDtypeStruct((2, 512, 640), BF)] * 2,
        in_specs=[pl.BlockSpec(memory_space=pltpu.SMEM)] + [away] * 11 + [whole] * len(args),
        out_specs=[away] * 2,
        scratch_shapes=[
            pltpu.VMEM((2, 512, 640), BF),
            pltpu.VMEM((2, 512, 640), BF),
            pltpu.VMEM((256, 4096), BF),
            pltpu.VMEM((4096, 256), BF),
            pltpu.VMEM((256, 4096), BF),
            pltpu.VMEM((2, 5, 512, 128), F32),
            pltpu.VMEM((5, 1024, 128), F32),
            pltpu.VMEM((1024, 640), BF),
            pltpu.VMEM((160, 4096), BF),
            pltpu.VMEM((2, 512, 640), BF),
            pltpu.VMEM((2, 512, 640), BF),
            pltpu.SemaphoreType.DMA((9,)),
            pltpu.SemaphoreType.DMA((20,)),
        ],
        compiler_params=params(),
        name="layer",
    )(place, own, other, *left, *right, x_rows, *args)


def shifted(item, axis):
    return [item] + [
        lax.ppermute(item, axis, [(i, (i + by) % 4) for i in range(4)]) for by in (1, 2, 3)
    ]


def hop(item, axis, by):
    pairs = [
        (4 * core + i, 4 * core + (i + (by if core == 0 else -by)) % 4)
        for core in range(2)
        for i in range(4)
    ]
    return lax.ppermute(item, ("co", axis), pairs)


def near_two(item, axis):
    return [hop(item, axis, by) for by in (1, 3)]


def across(back, axis):
    return hop(back, axis, 1)


def swap_core(item):
    return lax.ppermute(item, "co", [(0, 1), (1, 0)])


def mixers(order):
    block = jnp.arange(512, dtype=jnp.int32)

    def build(left, right):
        both = (left >> 3) & (right >> 3)
        both = both ^ (both >> 4)
        both = both ^ (both >> 2)
        both = both ^ (both >> 1)
        sign = 1 - 2 * (both & 1)
        return jnp.where((left & 7) == (right & 7), sign, 0).astype(BF)

    return build(order[:, None], block[None, :]), build(block[:, None], order[None, :])


def on_device(
    tokens,
    cotangent,
    gate_base,
    up_base,
    out_base,
    subspace,
    sign_flips,
    fast_gains,
    fast_scales,
    block_orders,
):
    const = tables()
    which, core = lax.axis_index("zh"), lax.axis_index("co")
    place = jnp.stack([which, core]).astype(jnp.int32)
    signs = sign_flips.reshape(2, 1024, 640)

    both, place = lax.optimization_barrier((jnp.concatenate([tokens, cotangent], axis=0), place))
    slots = shifted(both, "zl")
    first = lift_call(place, subspace, signs, const["half"])
    left, right = part_call(slots, const["apart"], const["columns"])
    first, left, right = lax.optimization_barrier((first, left, right))
    left_near, right_near = near_two(left, "x"), near_two(right, "y")
    block_orders, fast_gains, *left_near = lax.optimization_barrier(
        (block_orders, fast_gains, *left_near)
    )
    order = lax.dynamic_index_in_dim(block_orders, which, 0, keepdims=False)
    forward, adjoint = mixers(order)
    gains = lax.dynamic_slice(fast_gains, (which, 0, core, 0), (1, 512, 1, 640)).reshape(512, 640)
    left_far, right_far = across(left_near[0], "x"), across(right_near[0], "y")
    left_far, right_far, forward, adjoint, gains = lax.optimization_barrier(
        (left_far, right_far, forward, adjoint, gains)
    )
    left, right = join_call(
        [left, left_near[0], left_far, left_near[1]],
        [right, right_near[0], right_far, right_near[1]],
    )
    stage = (left, right)
    left_near, right_near = near_two(left, "y"), near_two(right, "x")
    first = lax.all_to_all(first.reshape(64, 8, 640), FSDP, split_axis=0, concat_axis=0, tiled=True)

    h512 = const["h512"]
    second = middle_call(forward, gains, h512, first.reshape(512, 640), stage)
    _, left_near, right_near, bases = lax.optimization_barrier(
        (second, left_near, right_near, (gate_base.T, up_base.T, out_base))
    )
    second = lax.all_to_all(
        second.reshape(128, 8, 640), HALVES, split_axis=0, concat_axis=0, tiled=True
    ).reshape(2, 512, 640)
    left = [left, left_near[0], across(left_near[0], "y"), left_near[1]]
    right = [right, right_near[0], across(right_near[0], "x"), right_near[1]]
    sorted_bases = sort_call(*bases, const["order"], const["columns"])
    prepared = base_call(left, right, *sorted_bases, const["unit"])
    second, *prepared = lax.optimization_barrier((second, *prepared))
    other = swap_core(second)
    keep, send = layer_call(
        place,
        second,
        other,
        left,
        right,
        prepared[0],
        const["pair"],
        const["pair_t"],
        fast_scales,
        const["window"],
        *prepared[1:],
    )
    backs = (keep.astype(F32) + swap_core(send).astype(F32)).astype(BF)
    backs = lax.all_to_all(
        backs.reshape(128, 8, 640), HALVES, split_axis=0, concat_axis=0, tiled=True
    ).reshape(2, 512, 640)
    folded = revert_call(adjoint, gains, h512, backs)
    folded = lax.all_to_all(
        folded.reshape(64, 8, 640), FSDP, split_axis=0, concat_axis=0, tiled=True
    )
    part = land_call(place, signs, const["half_t"], folded.reshape(512, 640))
    part = part + swap_core(part)
    return part + lax.ppermute(part, "zh", [(0, 1), (1, 0)])


def solution(mesh):
    split = Mesh(mesh.devices.reshape(2, 2, 4, 4, 4), AXES)
    group = ("zh", "co")
    in_specs = (
        P(group + FSDP, None),
        P(group + FSDP, None),
        P(None, FSDP),
        P(None, FSDP),
        P(FSDP, None),
        P(FSDP, None),
        P(None, FSDP, None, None),
        P(None, None, FSDP, None),
        P(None, FSDP, None),
        P(),
    )
    return jax.shard_map(
        on_device, mesh=split, in_specs=in_specs, out_specs=P(FSDP, None), check_vma=False
    )
```

```python
import functools

import jax
import jax.numpy as jnp
import numpy as np
from jax import lax
from jax.experimental import pallas as pl
from jax.experimental.pallas import tpu as pltpu
from jax.sharding import Mesh, PartitionSpec as P

D = 4096
FF = 10240
BF = jnp.bfloat16
F32 = jnp.float32
AXES = ("zh", "co", "y", "x", "zl")
FSDP = ("y", "x", "zl")
HALVES = ("zh", "y", "x", "zl")
VMEM_BYTES = 60 * 1024 * 1024


def sylvester(size):
    matrix = np.ones((1, 1), np.float32)
    while matrix.shape[0] < size:
        matrix = np.block([[matrix, matrix], [matrix, -matrix]])
    return matrix


@functools.cache
def tables():
    h128, h512 = sylvester(128), sylvester(512)
    half = np.stack([h128[par::2] for par in range(2)])
    pair = np.stack([np.concatenate([h128[:, par::2], h128[:, 1 - par :: 2]], 1) for par in range(2)])
    hidden = np.arange(160)
    place = (hidden % 5) * 32 + hidden // 5
    window = np.zeros((4, 256, 160), np.float32)
    for q in range(4):
        window[q, 32 * q + hidden, place] = 1
    order = np.zeros((160, 160), np.float32)
    order[place, hidden] = 1
    columns = np.zeros((512, 512), np.float32)
    q, r = np.divmod(np.arange(512), 128)
    columns[np.arange(512), r * 4 + q] = 1
    apart = np.zeros((32, 32), np.float32)
    row = np.arange(16)
    apart[row, (row // 4) * 8 + row % 4] = 1
    apart[16 + row, (row // 4) * 8 + 4 + row % 4] = 1
    cast = lambda value: np.ascontiguousarray(value).astype(BF)
    return dict(
        half=cast(half),
        half_t=cast(half.transpose(0, 2, 1)),
        pair=cast(pair),
        pair_t=cast(pair.transpose(0, 2, 1)),
        h512=cast(h512),
        window=cast(window),
        order=cast(order),
        columns=cast(columns),
        apart=cast(apart),
        unit=cast(np.eye(256)),
    )


def butterfly(items):
    step = 1
    while step < len(items):
        items = [
            items[i] + items[i ^ step] if not i & step else items[i ^ step] - items[i]
            for i in range(len(items))
        ]
        step *= 2
    return items


def dot(left, right):
    return jnp.dot(left, right, preferred_element_type=F32)


def dot_t(left, right):
    return lax.dot_general(left, right, (((1,), (1,)), ((), ())), preferred_element_type=F32)


def dot_l(left, right):
    return lax.dot_general(left, right, (((0,), (0,)), ((), ())), preferred_element_type=F32)


def params():
    return pltpu.CompilerParams(vmem_limit_bytes=VMEM_BYTES)


def lift_kernel(place, sub, signs, half, out, flips, parts, rows, sems):
    copies = []
    for a in range(8):
        block = pl.ds(128 * a, 128)
        copies.append(pltpu.make_async_copy(signs.at[place[0], block], flips.at[block], sems.at[a]))
        copies[-1].start()
    grid = half[place[1]]
    for a in range(8):
        row = sub[a : a + 1, :]
        high = row.astype(BF)
        low = (row - high.astype(F32)).astype(BF)
        scaled = jnp.concatenate([grid * high, grid * low], axis=1)
        copies[a].wait()
        flip = flips[128 * a : 128 * (a + 1), :].astype(F32).astype(BF)
        parts[a] = dot(scaled, jnp.concatenate([flip, flip], axis=0))
    for kt in range(5):
        tile = slice(128 * kt, 128 * (kt + 1))
        for part in range(4):
            at = slice(16 * part, 16 * (part + 1))
            mixed = butterfly([parts[a, at, tile] for a in range(8)])
            for b in range(8):
                rows[kt, pl.ds(128 * part + b, 16, stride=8), :] = mixed[b]
    for kt in range(5):
        out[:, 128 * kt : 128 * (kt + 1)] = (rows[kt] * (1.0 / 32.0)).astype(BF)


def lift_call(place, subspace, signs, half):
    whole = pl.BlockSpec(memory_space=pltpu.VMEM)
    away = pl.BlockSpec(memory_space=pl.ANY)
    return pl.pallas_call(
        lift_kernel,
        out_shape=jax.ShapeDtypeStruct((512, 640), BF),
        in_specs=[pl.BlockSpec(memory_space=pltpu.SMEM), whole, away, whole],
        out_specs=whole,
        scratch_shapes=[
            pltpu.VMEM((1024, 640), jnp.int32),
            pltpu.VMEM((8, 64, 640), F32),
            pltpu.VMEM((5, 512, 128), F32),
            pltpu.SemaphoreType.DMA((8,)),
        ],
        compiler_params=params(),
        name="lift",
    )(place, subspace, signs, half)


def middle_kernel(mixer, gains, h512, first, *rest):
    out = rest[-1]
    turned = dot(mixer[...], first[...]) * 0.125
    mixed = (gains[...].astype(F32) * turned).astype(BF)
    second = (dot(h512[...], mixed) * 512**-0.5).astype(BF)
    out[0] = second
    out[1] = second


def middle_call(mixer, gains, h512, first, after=()):
    whole = pl.BlockSpec(memory_space=pltpu.VMEM)
    away = pl.BlockSpec(memory_space=pl.ANY)
    return pl.pallas_call(
        middle_kernel,
        out_shape=jax.ShapeDtypeStruct((2, 512, 640), BF),
        in_specs=[whole] * 4 + [away] * len(after),
        out_specs=whole,
        compiler_params=params(),
        name="middle",
    )(mixer, gains, h512, first, *after)


def revert_kernel(mixer, gains, h512, backs, out):
    spread = (dot(h512[...], backs[0]) + dot(h512[...], backs[1])) * 512**-0.5
    spread = (gains[...].astype(F32) * spread).astype(BF)
    out[...] = (dot(mixer[...], spread) * 0.125).astype(BF)


def revert_call(mixer, gains, h512, backs):
    return pl.pallas_call(
        revert_kernel,
        out_shape=jax.ShapeDtypeStruct((512, 640), BF),
        compiler_params=params(),
        name="revert",
    )(mixer, gains, h512, backs)


def land_kernel(place, signs, half_t, folded, out, flips, rows, parts, sems):
    copies = []
    for a in range(8):
        block = pl.ds(128 * a, 128)
        copies.append(pltpu.make_async_copy(signs.at[place[0], block], flips.at[block], sems.at[a]))
        copies[-1].start()
    grid = half_t[place[1]]
    for kt in range(5):
        rows[kt] = folded[:, 128 * kt : 128 * (kt + 1)].astype(F32)
    for a in range(8):
        block = [rows[kt, pl.ds(a, 64, stride=8), :] for kt in range(5)]
        parts[a] = dot(grid, jnp.concatenate(block, axis=1).astype(BF))
    for copy in copies:
        copy.wait()
    ones = jnp.ones((8, 128), BF)
    for part in range(8):
        at = slice(16 * part, 16 * (part + 1))
        lanes = [None] * 8
        for kt in range(5):
            tile = slice(128 * kt, 128 * (kt + 1))
            mixed = butterfly([parts[a, at, tile] for a in range(8)])
            for b in range(8):
                start = 128 * b + 16 * part
                term = mixed[b] * flips[start : start + 16, tile].astype(F32)
                lanes[b] = term if lanes[b] is None else lanes[b] + term
        for b in range(8):
            parts[b, at, 0:128] = lanes[b]
    for b in range(8):
        full = parts[b, :, 0:128]
        high = full.astype(BF)
        rest = full - high.astype(F32)
        low = rest.astype(BF)
        last = (rest - low.astype(F32)).astype(BF)
        sums = dot_t(ones, high) + dot_t(ones, low) + dot_t(ones, last)
        out[b : b + 1, :] = sums[0:1, :] * (1.0 / 32.0)


def land_call(place, signs, half_t, folded):
    whole = pl.BlockSpec(memory_space=pltpu.VMEM)
    away = pl.BlockSpec(memory_space=pl.ANY)
    return pl.pallas_call(
        land_kernel,
        out_shape=jax.ShapeDtypeStruct((8, 128), F32),
        in_specs=[pl.BlockSpec(memory_space=pltpu.SMEM), away, whole, whole],
        out_specs=whole,
        scratch_shapes=[
            pltpu.VMEM((1024, 640), jnp.int32),
            pltpu.VMEM((5, 512, 128), F32),
            pltpu.VMEM((8, 128, 640), F32),
            pltpu.SemaphoreType.DMA((8,)),
        ],
        compiler_params=params(),
        name="land",
    )(place, signs, half_t, folded)


def sort_columns(item, columns, target):
    height = item.shape[0]
    stack = jnp.concatenate([item[:, 512 * g : 512 * (g + 1)] for g in range(8)], axis=0)
    stack = dot_t(stack, columns).astype(BF)
    for g in range(8):
        for q in range(4):
            at = 1024 * q + 128 * g
            target[:, at : at + 128] = stack[height * g : height * (g + 1), 128 * q : 128 * (q + 1)]


def part_kernel(a, b, c, d, order, columns, left, right):
    stack = jnp.concatenate([item[...].astype(F32) for item in (a, b, c, d)], axis=0).astype(BF)
    apart = dot(order[...], stack).astype(BF)
    sort_columns(apart[0:16, :], columns[...], left)
    right[...] = apart[16:32, :]


def part_call(slots, order, columns):
    return pl.pallas_call(
        part_kernel,
        out_shape=[jax.ShapeDtypeStruct((16, 4096), BF)] * 2,
        compiler_params=params(),
        name="part",
    )(*slots, order, columns)


def join_kernel(*refs):
    ins, outs = refs[:8], refs[8:10]
    for i in range(8):
        outs[i // 4][16 * (i % 4) : 16 * (i % 4) + 16, :] = ins[i][...]


JOIN_COST = 10**10


def join_call(left, right):
    return pl.pallas_call(
        join_kernel,
        out_shape=[jax.ShapeDtypeStruct((64, 4096), BF)] * 2,
        compiler_params=params(),
        cost_estimate=pl.CostEstimate(flops=JOIN_COST, bytes_accessed=10**6, transcendentals=0),
        name="join",
    )(*left, *right)


def sort_kernel(gate_base, up_base, out_base, order, columns, gate, up, out):
    for base, target in ((gate_base, gate), (up_base, up)):
        ordered = dot(order[...], base[...]).astype(BF)
        for g in range(8):
            turned = dot_t(columns[...], ordered[:, 512 * g : 512 * (g + 1)]).astype(BF)
            for q in range(4):
                at = 1024 * q + 128 * g
                target[at : at + 128, :] = turned[128 * q : 128 * (q + 1), :]
    out[...] = jnp.transpose(dot(order[...], out_base[...])).astype(BF)


def sort_call(*args):
    return pl.pallas_call(
        sort_kernel,
        out_shape=[jax.ShapeDtypeStruct((4096, 160), BF)] * 3,
        compiler_params=params(),
        name="sort",
    )(*args)


def collect(left, right, x, dy, sems):
    copies = [pltpu.make_async_copy(left[i], x.at[pl.ds(64 * i, 64)], sems.at[i]) for i in range(4)]
    late = [
        pltpu.make_async_copy(
            right[i].at[pl.ds(16 * j, 16)], dy.at[pl.ds(64 * j + 16 * i, 16)], sems.at[4 + 4 * i + j]
        )
        for i in range(4)
        for j in range(4)
    ]
    for copy in copies + late:
        copy.start()
    return copies, late


def base_kernel(*refs):
    left, right = refs[0:4], refs[4:8]
    bases, unit = refs[8:11], refs[11]
    x_rows_far, gate, up, grad = refs[12:16]
    x, dy, near, x_rows, sems, piece_sems = refs[16:22]
    loads = [pltpu.make_async_copy(bases[i], near.at[i], sems.at[i]) for i in range(3)]
    loads[0].start()
    first, late = collect(left, right, x, dy, piece_sems)
    for load in loads[1:]:
        load.start()
    for copy in first:
        copy.wait()
    loads[0].wait()
    gate[...] = dot(x[...], near[0])
    leaves = []
    for part in range(4):
        for g in range(4 * part, 4 * (part + 1)):
            at = slice(256 * g, 256 * (g + 1))
            x_rows[at, :] = dot_t(unit[...], x[:, at]).astype(BF)
        rows = pl.ds(1024 * part, 1024)
        leaves.append(
            pltpu.make_async_copy(x_rows.at[rows], x_rows_far.at[rows], sems.at[3 + part])
        )
        leaves[-1].start()
    loads[1].wait()
    up[...] = dot(x[...], near[1])
    for copy in late:
        copy.wait()
    loads[2].wait()
    grad[...] = dot(dy[...], near[2])
    for leave in leaves:
        leave.wait()


COST = 2 * 10**10


def base_call(left, right, gate_base, up_base, out_base, unit):
    whole = pl.BlockSpec(memory_space=pltpu.VMEM)
    away = pl.BlockSpec(memory_space=pl.ANY)
    return pl.pallas_call(
        base_kernel,
        out_shape=[jax.ShapeDtypeStruct((4096, 256), BF)]
        + [jax.ShapeDtypeStruct((256, 160), F32)] * 3,
        in_specs=[away] * 11 + [whole],
        out_specs=[away] + [whole] * 3,
        scratch_shapes=[
            pltpu.VMEM((256, 4096), BF),
            pltpu.VMEM((256, 4096), BF),
            pltpu.VMEM((3, 4096, 160), BF),
            pltpu.VMEM((4096, 256), BF),
            pltpu.SemaphoreType.DMA((7,)),
            pltpu.SemaphoreType.DMA((20,)),
        ],
        compiler_params=params(),
        cost_estimate=pl.CostEstimate(flops=COST, bytes_accessed=10**6, transcendentals=0),
        name="base",
    )(*left, *right, gate_base, up_base, out_base, unit)


def layer_kernel(
    place,
    own_far,
    other_far,
    l0,
    l1,
    l2,
    l3,
    r0,
    r1,
    r2,
    r3,
    x_rows_far,
    pair,
    pair_t,
    scales,
    window,
    gate_part,
    up_part,
    grad_part,
    keep_far,
    send_far,
    own,
    other,
    x_cols,
    x_rows,
    dy,
    near,
    tall,
    e0,
    w1,
    keep,
    send,
    sems,
    piece_sems,
):
    mine = place[1]
    count = [0]
    waits = {}

    def bring(key, source, target):
        copy = pltpu.make_async_copy(source, target, sems.at[count[0]])
        count[0] += 1
        copy.start()
        waits[key] = copy

    for m in range(2):
        bring(("own", m), own_far.at[m], own.at[m])
        bring(("other", m), other_far.at[m], other.at[m])
    first, late = collect((l0, l1, l2, l3), (r0, r1, r2, r3), x_cols, dy, piece_sems)
    bring("x_rows", x_rows_far, x_rows)

    factors = ((D**-0.5) * (128**-0.5), (FF**-0.5) * (128**-0.5))
    tiles = [slice(128 * kt, 128 * (kt + 1)) for kt in range(5)]
    grid, grid_t = pair[mine], pair_t[mine]

    def widen(m, put):
        waits[("own", m)].wait()
        waits[("other", m)].wait()
        for kt in range(5):
            near[0, kt] = own[m, :, tiles[kt]].astype(F32)
            near[1, kt] = other[m, :, tiles[kt]].astype(F32)
        for b in range(8):
            block = jnp.concatenate(
                [
                    jnp.concatenate(
                        [near[side, kt, pl.ds(b, 64, stride=8), :] for kt in range(5)], axis=1
                    )
                    for side in range(2)
                ],
                axis=0,
            ).astype(BF)
            put(b, dot(grid, block) * (scales[m, b : b + 1, :] * factors[m]))

    def put0(b, wide):
        e0[128 * b : 128 * (b + 1), :] = wide.astype(BF)

    def put1(b, wide):
        for kt in range(5):
            tall[kt, 128 * b : 128 * (b + 1), :] = wide[:, tiles[kt]]

    widen(0, put0)
    widen(1, put1)
    for w in range(32):
        for kt in range(5):
            v, jt = divmod(5 * w + kt, 32)
            w1[32 * v : 32 * (v + 1), 128 * jt : 128 * (jt + 1)] = tall[
                kt, pl.ds(w, 32, stride=32), :
            ].astype(BF)
    for copy in first + late + [waits["x_rows"]]:
        copy.wait()
    gate = gate_part[...]
    for q in range(4):
        part = dot(x_cols[:, 1024 * q : 1024 * (q + 1)], e0[:, 128 * q : 128 * q + 256])
        high = part.astype(BF)
        low = (part - high.astype(F32)).astype(BF)
        gate = gate + dot(high, window[q]) + dot(low, window[q])
    up = up_part[...]
    grad = grad_part[...] + dot_t(dy[...], w1[...])
    argument = 0.7978845608028654 * (gate + 0.044715 * gate * gate * gate)
    tangent = jnp.tanh(argument)
    half = 0.5 * (1.0 + tangent)
    hidden = (gate * half * up).astype(BF)
    slope = half + 0.5 * gate * (1.0 - tangent * tangent) * 0.7978845608028654 * (
        1.0 + 0.134145 * gate * gate
    )
    gate_grad = (grad * up * slope).astype(BF)
    out_grad = dot_l(hidden, dy[...])
    for w in range(32):
        for kt in range(5):
            v, jt = divmod(5 * w + kt, 32)
            tall[kt, pl.ds(w, 32, stride=32), :] = out_grad[
                32 * v : 32 * (v + 1), 128 * jt : 128 * (jt + 1)
            ]

    def leave(m, get):
        for b in range(8):
            back = dot(grid_t, (get(b) * (scales[m, b : b + 1, :] * factors[m])).astype(BF))
            for kt in range(5):
                near[0, kt, pl.ds(b, 64, stride=8), :] = back[0:64, tiles[kt]]
                near[1, kt, pl.ds(b, 64, stride=8), :] = back[64:128, tiles[kt]]
        for kt in range(5):
            send[m, :, tiles[kt]] = near[1, kt].astype(BF)
            keep[m, :, tiles[kt]] = near[0, kt].astype(BF)
        bring(("send", m), send.at[m], send_far.at[m])
        bring(("keep", m), keep.at[m], keep_far.at[m])

    def rows_of(b):
        return jnp.concatenate([tall[kt, 128 * b : 128 * (b + 1), :] for kt in range(5)], axis=1)

    leave(1, rows_of)
    windows = [dot_t(gate_grad, window[q]).astype(BF) for q in range(4)]

    for q in range(4):
        part = dot(x_rows[1024 * q : 1024 * (q + 1), :], windows[q])
        tall[q] = part[:, 0:128] + tall[q] if q else part[:, 0:128]
        tall[q + 1] = part[:, 128:256]

    leave(0, rows_of)
    for m in range(2):
        for side in ("send", "keep"):
            waits[(side, m)].wait()


def layer_call(place, own, other, left, right, x_rows, *args):
    whole = pl.BlockSpec(memory_space=pltpu.VMEM)
    away = pl.BlockSpec(memory_space=pl.ANY)
    return pl.pallas_call(
        layer_kernel,
        out_shape=[jax.ShapeDtypeStruct((2, 512, 640), BF)] * 2,
        in_specs=[pl.BlockSpec(memory_space=pltpu.SMEM)] + [away] * 11 + [whole] * len(args),
        out_specs=[away] * 2,
        scratch_shapes=[
            pltpu.VMEM((2, 512, 640), BF),
            pltpu.VMEM((2, 512, 640), BF),
            pltpu.VMEM((256, 4096), BF),
            pltpu.VMEM((4096, 256), BF),
            pltpu.VMEM((256, 4096), BF),
            pltpu.VMEM((2, 5, 512, 128), F32),
            pltpu.VMEM((5, 1024, 128), F32),
            pltpu.VMEM((1024, 640), BF),
            pltpu.VMEM((160, 4096), BF),
            pltpu.VMEM((2, 512, 640), BF),
            pltpu.VMEM((2, 512, 640), BF),
            pltpu.SemaphoreType.DMA((9,)),
            pltpu.SemaphoreType.DMA((20,)),
        ],
        compiler_params=params(),
        name="layer",
    )(place, own, other, *left, *right, x_rows, *args)


def shifted(item, axis):
    return [item] + [
        lax.ppermute(item, axis, [(i, (i + by) % 4) for i in range(4)]) for by in (1, 2, 3)
    ]


def hop(item, axis, by):
    pairs = [
        (4 * core + i, 4 * core + (i + (by if core == 0 else -by)) % 4)
        for core in range(2)
        for i in range(4)
    ]
    return lax.ppermute(item, ("co", axis), pairs)


def near_two(item, axis):
    return [hop(item, axis, by) for by in (1, 3)]


def across(back, axis):
    return hop(back, axis, 1)


def swap_core(item):
    return lax.ppermute(item, "co", [(0, 1), (1, 0)])


def mixers(order):
    block = jnp.arange(512, dtype=jnp.int32)

    def build(left, right):
        both = (left >> 3) & (right >> 3)
        both = both ^ (both >> 4)
        both = both ^ (both >> 2)
        both = both ^ (both >> 1)
        sign = 1 - 2 * (both & 1)
        return jnp.where((left & 7) == (right & 7), sign, 0).astype(BF)

    return build(order[:, None], block[None, :]), build(block[:, None], order[None, :])


def on_device(
    tokens,
    cotangent,
    gate_base,
    up_base,
    out_base,
    subspace,
    sign_flips,
    fast_gains,
    fast_scales,
    block_orders,
):
    const = tables()
    which, core = lax.axis_index("zh"), lax.axis_index("co")
    place = jnp.stack([which, core]).astype(jnp.int32)
    signs = sign_flips.reshape(2, 1024, 640)

    both, place = lax.optimization_barrier((jnp.concatenate([tokens, cotangent], axis=0), place))
    slots = shifted(both, "zl")
    first = lift_call(place, subspace, signs, const["half"])
    left, right = part_call(slots, const["apart"], const["columns"])
    first, left, right = lax.optimization_barrier((first, left, right))
    left_near, right_near = near_two(left, "x"), near_two(right, "y")
    block_orders, fast_gains, *left_near = lax.optimization_barrier(
        (block_orders, fast_gains, *left_near)
    )
    order = lax.dynamic_index_in_dim(block_orders, which, 0, keepdims=False)
    forward, adjoint = mixers(order)
    gains = lax.dynamic_slice(fast_gains, (which, 0, core, 0), (1, 512, 1, 640)).reshape(512, 640)
    left_far, right_far = across(left_near[0], "x"), across(right_near[0], "y")
    left_far, right_far, forward, adjoint, gains = lax.optimization_barrier(
        (left_far, right_far, forward, adjoint, gains)
    )
    left, right = join_call(
        [left, left_near[0], left_far, left_near[1]],
        [right, right_near[0], right_far, right_near[1]],
    )
    stage = (left, right)
    left_near, right_near = near_two(left, "y"), near_two(right, "x")
    first = lax.all_to_all(first.reshape(64, 8, 640), FSDP, split_axis=0, concat_axis=0, tiled=True)

    h512 = const["h512"]
    second = middle_call(forward, gains, h512, first.reshape(512, 640), stage)
    _, left_near, right_near, bases = lax.optimization_barrier(
        (second, left_near, right_near, (gate_base.T, up_base.T, out_base))
    )
    second = lax.all_to_all(
        second.reshape(128, 8, 640), HALVES, split_axis=0, concat_axis=0, tiled=True
    ).reshape(2, 512, 640)
    left = [left, left_near[0], across(left_near[0], "y"), left_near[1]]
    right = [right, right_near[0], across(right_near[0], "x"), right_near[1]]
    sorted_bases = sort_call(*bases, const["order"], const["columns"])
    prepared = base_call(left, right, *sorted_bases, const["unit"])
    second, *prepared = lax.optimization_barrier((second, *prepared))
    other = swap_core(second)
    keep, send = layer_call(
        place,
        second,
        other,
        left,
        right,
        prepared[0],
        const["pair"],
        const["pair_t"],
        fast_scales,
        const["window"],
        *prepared[1:],
    )
    backs = (keep.astype(F32) + swap_core(send).astype(F32)).astype(BF)
    backs = lax.all_to_all(
        backs.reshape(128, 8, 640), HALVES, split_axis=0, concat_axis=0, tiled=True
    ).reshape(2, 512, 640)
    folded = revert_call(adjoint, gains, h512, backs)
    folded = lax.all_to_all(
        folded.reshape(64, 8, 640), FSDP, split_axis=0, concat_axis=0, tiled=True
    )
    part = land_call(place, signs, const["half_t"], folded.reshape(512, 640))
    part = part + swap_core(part)
    return part + lax.ppermute(part, "zh", [(0, 1), (1, 0)])


def solution(mesh):
    split = Mesh(mesh.devices.reshape(2, 2, 4, 4, 4), AXES)
    group = ("zh", "co")
    in_specs = (
        P(group + FSDP, None),
        P(group + FSDP, None),
        P(None, FSDP),
        P(None, FSDP),
        P(FSDP, None),
        P(FSDP, None),
        P(None, FSDP, None, None),
        P(None, None, FSDP, None),
        P(None, FSDP, None),
        P(),
    )
    return jax.shard_map(
        on_device, mesh=split, in_specs=in_specs, out_specs=P(FSDP, None), check_vma=False
    )
```

```python
import functools

import jax
import jax.numpy as jnp
import numpy as np
from jax import lax
from jax.experimental import pallas as pl
from jax.experimental.pallas import tpu as pltpu
from jax.sharding import Mesh, PartitionSpec as P

D = 4096
FF = 10240
BF = jnp.bfloat16
F32 = jnp.float32
AXES = ("zh", "co", "y", "x", "zl")
FSDP = ("y", "x", "zl")
HALVES = ("zh", "y", "x", "zl")
VMEM_BYTES = 60 * 1024 * 1024


def sylvester(size):
    matrix = np.ones((1, 1), np.float32)
    while matrix.shape[0] < size:
        matrix = np.block([[matrix, matrix], [matrix, -matrix]])
    return matrix


@functools.cache
def tables():
    h128, h512 = sylvester(128), sylvester(512)
    half = np.stack([h128[par::2] for par in range(2)])
    pair = np.stack([np.concatenate([h128[:, par::2], h128[:, 1 - par :: 2]], 1) for par in range(2)])
    hidden = np.arange(160)
    place = (hidden % 5) * 32 + hidden // 5
    window = np.zeros((4, 256, 160), np.float32)
    for q in range(4):
        window[q, 32 * q + hidden, place] = 1
    order = np.zeros((160, 160), np.float32)
    order[place, hidden] = 1
    columns = np.zeros((512, 512), np.float32)
    q, r = np.divmod(np.arange(512), 128)
    columns[np.arange(512), r * 4 + q] = 1
    apart = np.zeros((32, 32), np.float32)
    row = np.arange(16)
    apart[row, (row // 4) * 8 + row % 4] = 1
    apart[16 + row, (row // 4) * 8 + 4 + row % 4] = 1
    cast = lambda value: np.ascontiguousarray(value).astype(BF)
    return dict(
        half=cast(half),
        half_t=cast(half.transpose(0, 2, 1)),
        pair=cast(pair),
        pair_t=cast(pair.transpose(0, 2, 1)),
        h512=cast(h512),
        window=cast(window),
        order=cast(order),
        columns=cast(columns),
        apart=cast(apart),
        unit=cast(np.eye(256)),
    )


def butterfly(items):
    step = 1
    while step < len(items):
        items = [
            items[i] + items[i ^ step] if not i & step else items[i ^ step] - items[i]
            for i in range(len(items))
        ]
        step *= 2
    return items


def dot(left, right):
    return jnp.dot(left, right, preferred_element_type=F32)


def dot_t(left, right):
    return lax.dot_general(left, right, (((1,), (1,)), ((), ())), preferred_element_type=F32)


def dot_l(left, right):
    return lax.dot_general(left, right, (((0,), (0,)), ((), ())), preferred_element_type=F32)


def params():
    return pltpu.CompilerParams(vmem_limit_bytes=VMEM_BYTES)


def lift_kernel(place, sub, signs, half, out, flips, parts, rows, sems):
    copies = []
    for a in range(8):
        block = pl.ds(128 * a, 128)
        copies.append(pltpu.make_async_copy(signs.at[place[0], block], flips.at[block], sems.at[a]))
        copies[-1].start()
    grid = half[place[1]]
    for a in range(8):
        row = sub[a : a + 1, :]
        high = row.astype(BF)
        low = (row - high.astype(F32)).astype(BF)
        scaled = jnp.concatenate([grid * high, grid * low], axis=1)
        copies[a].wait()
        flip = flips[128 * a : 128 * (a + 1), :].astype(F32).astype(BF)
        parts[a] = dot(scaled, jnp.concatenate([flip, flip], axis=0))
    for kt in range(5):
        tile = slice(128 * kt, 128 * (kt + 1))
        for part in range(4):
            at = slice(16 * part, 16 * (part + 1))
            mixed = butterfly([parts[a, at, tile] for a in range(8)])
            for b in range(8):
                rows[kt, pl.ds(128 * part + b, 16, stride=8), :] = mixed[b]
    for kt in range(5):
        out[:, 128 * kt : 128 * (kt + 1)] = (rows[kt] * (1.0 / 32.0)).astype(BF)


def lift_call(place, subspace, signs, half):
    whole = pl.BlockSpec(memory_space=pltpu.VMEM)
    away = pl.BlockSpec(memory_space=pl.ANY)
    return pl.pallas_call(
        lift_kernel,
        out_shape=jax.ShapeDtypeStruct((512, 640), BF),
        in_specs=[pl.BlockSpec(memory_space=pltpu.SMEM), whole, away, whole],
        out_specs=whole,
        scratch_shapes=[
            pltpu.VMEM((1024, 640), jnp.int32),
            pltpu.VMEM((8, 64, 640), F32),
            pltpu.VMEM((5, 512, 128), F32),
            pltpu.SemaphoreType.DMA((8,)),
        ],
        compiler_params=params(),
        name="lift",
    )(place, subspace, signs, half)


def middle_kernel(mixer, gains, h512, first, *rest):
    out = rest[-1]
    turned = dot(mixer[...], first[...]) * 0.125
    mixed = (gains[...].astype(F32) * turned).astype(BF)
    second = (dot(h512[...], mixed) * 512**-0.5).astype(BF)
    out[0] = second
    out[1] = second


def middle_call(mixer, gains, h512, first, after=()):
    whole = pl.BlockSpec(memory_space=pltpu.VMEM)
    away = pl.BlockSpec(memory_space=pl.ANY)
    return pl.pallas_call(
        middle_kernel,
        out_shape=jax.ShapeDtypeStruct((2, 512, 640), BF),
        in_specs=[whole] * 4 + [away] * len(after),
        out_specs=whole,
        compiler_params=params(),
        name="middle",
    )(mixer, gains, h512, first, *after)


def revert_kernel(mixer, gains, h512, backs, out):
    spread = (dot(h512[...], backs[0]) + dot(h512[...], backs[1])) * 512**-0.5
    spread = (gains[...].astype(F32) * spread).astype(BF)
    out[...] = (dot(mixer[...], spread) * 0.125).astype(BF)


def revert_call(mixer, gains, h512, backs):
    return pl.pallas_call(
        revert_kernel,
        out_shape=jax.ShapeDtypeStruct((512, 640), BF),
        compiler_params=params(),
        name="revert",
    )(mixer, gains, h512, backs)


def land_kernel(place, signs, half_t, folded, out, flips, rows, parts, sems):
    copies = []
    for a in range(8):
        block = pl.ds(128 * a, 128)
        copies.append(pltpu.make_async_copy(signs.at[place[0], block], flips.at[block], sems.at[a]))
        copies[-1].start()
    grid = half_t[place[1]]
    for kt in range(5):
        rows[kt] = folded[:, 128 * kt : 128 * (kt + 1)].astype(F32)
    for a in range(8):
        block = [rows[kt, pl.ds(a, 64, stride=8), :] for kt in range(5)]
        parts[a] = dot(grid, jnp.concatenate(block, axis=1).astype(BF))
    for copy in copies:
        copy.wait()
    ones = jnp.ones((8, 128), BF)
    for part in range(8):
        at = slice(16 * part, 16 * (part + 1))
        lanes = [None] * 8
        for kt in range(5):
            tile = slice(128 * kt, 128 * (kt + 1))
            mixed = butterfly([parts[a, at, tile] for a in range(8)])
            for b in range(8):
                start = 128 * b + 16 * part
                term = mixed[b] * flips[start : start + 16, tile].astype(F32)
                lanes[b] = term if lanes[b] is None else lanes[b] + term
        for b in range(8):
            parts[b, at, 0:128] = lanes[b]
    for b in range(8):
        full = parts[b, :, 0:128]
        high = full.astype(BF)
        rest = full - high.astype(F32)
        low = rest.astype(BF)
        last = (rest - low.astype(F32)).astype(BF)
        sums = dot_t(ones, high) + dot_t(ones, low) + dot_t(ones, last)
        out[b : b + 1, :] = sums[0:1, :] * (1.0 / 32.0)


def land_call(place, signs, half_t, folded):
    whole = pl.BlockSpec(memory_space=pltpu.VMEM)
    away = pl.BlockSpec(memory_space=pl.ANY)
    return pl.pallas_call(
        land_kernel,
        out_shape=jax.ShapeDtypeStruct((8, 128), F32),
        in_specs=[pl.BlockSpec(memory_space=pltpu.SMEM), away, whole, whole],
        out_specs=whole,
        scratch_shapes=[
            pltpu.VMEM((1024, 640), jnp.int32),
            pltpu.VMEM((5, 512, 128), F32),
            pltpu.VMEM((8, 128, 640), F32),
            pltpu.SemaphoreType.DMA((8,)),
        ],
        compiler_params=params(),
        name="land",
    )(place, signs, half_t, folded)


def sort_columns(item, columns, target):
    height = item.shape[0]
    stack = jnp.concatenate([item[:, 512 * g : 512 * (g + 1)] for g in range(8)], axis=0)
    stack = dot_t(stack, columns).astype(BF)
    for g in range(8):
        for q in range(4):
            at = 1024 * q + 128 * g
            target[:, at : at + 128] = stack[height * g : height * (g + 1), 128 * q : 128 * (q + 1)]


def part_kernel(a, b, c, d, order, columns, left, right):
    stack = jnp.concatenate([item[...].astype(F32) for item in (a, b, c, d)], axis=0).astype(BF)
    apart = dot(order[...], stack).astype(BF)
    sort_columns(apart[0:16, :], columns[...], left)
    right[...] = apart[16:32, :]


def part_call(slots, order, columns):
    return pl.pallas_call(
        part_kernel,
        out_shape=[jax.ShapeDtypeStruct((16, 4096), BF)] * 2,
        compiler_params=params(),
        name="part",
    )(*slots, order, columns)


def join_kernel(*refs):
    ins, outs = refs[:8], refs[8:10]
    for i in range(8):
        outs[i // 4][16 * (i % 4) : 16 * (i % 4) + 16, :] = ins[i][...]


JOIN_COST = 10**10


def join_call(left, right):
    return pl.pallas_call(
        join_kernel,
        out_shape=[jax.ShapeDtypeStruct((64, 4096), BF)] * 2,
        compiler_params=params(),
        cost_estimate=pl.CostEstimate(flops=JOIN_COST, bytes_accessed=10**6, transcendentals=0),
        name="join",
    )(*left, *right)


def sort_kernel(gate_base, up_base, out_base, order, columns, gate, up, out):
    for base, target in ((gate_base, gate), (up_base, up)):
        ordered = dot(order[...], base[...]).astype(BF)
        for g in range(8):
            turned = dot_t(columns[...], ordered[:, 512 * g : 512 * (g + 1)]).astype(BF)
            for q in range(4):
                at = 1024 * q + 128 * g
                target[at : at + 128, :] = turned[128 * q : 128 * (q + 1), :]
    out[...] = jnp.transpose(dot(order[...], out_base[...])).astype(BF)


def sort_call(*args):
    return pl.pallas_call(
        sort_kernel,
        out_shape=[jax.ShapeDtypeStruct((4096, 160), BF)] * 3,
        compiler_params=params(),
        name="sort",
    )(*args)


def collect(left, right, x, dy, sems):
    copies = [pltpu.make_async_copy(left[i], x.at[pl.ds(64 * i, 64)], sems.at[i]) for i in range(4)]
    late = [
        pltpu.make_async_copy(
            right[i].at[pl.ds(16 * j, 16)], dy.at[pl.ds(64 * j + 16 * i, 16)], sems.at[4 + 4 * i + j]
        )
        for i in range(4)
        for j in range(4)
    ]
    for copy in copies + late:
        copy.start()
    return copies, late


def base_kernel(*refs):
    left, right = refs[0:4], refs[4:8]
    bases, unit = refs[8:11], refs[11]
    x_rows_far, gate, up, grad = refs[12:16]
    x, dy, near, x_rows, sems, piece_sems = refs[16:22]
    loads = [pltpu.make_async_copy(bases[i], near.at[i], sems.at[i]) for i in range(3)]
    loads[0].start()
    first, late = collect(left, right, x, dy, piece_sems)
    for load in loads[1:]:
        load.start()
    for copy in first:
        copy.wait()
    loads[0].wait()
    gate[...] = dot(x[...], near[0])
    leaves = []
    for part in range(4):
        for g in range(4 * part, 4 * (part + 1)):
            at = slice(256 * g, 256 * (g + 1))
            x_rows[at, :] = dot_t(unit[...], x[:, at]).astype(BF)
        rows = pl.ds(1024 * part, 1024)
        leaves.append(
            pltpu.make_async_copy(x_rows.at[rows], x_rows_far.at[rows], sems.at[3 + part])
        )
        leaves[-1].start()
    loads[1].wait()
    up[...] = dot(x[...], near[1])
    for copy in late:
        copy.wait()
    loads[2].wait()
    grad[...] = dot(dy[...], near[2])
    for leave in leaves:
        leave.wait()


COST = 2 * 10**10


def base_call(left, right, gate_base, up_base, out_base, unit):
    whole = pl.BlockSpec(memory_space=pltpu.VMEM)
    away = pl.BlockSpec(memory_space=pl.ANY)
    return pl.pallas_call(
        base_kernel,
        out_shape=[jax.ShapeDtypeStruct((4096, 256), BF)]
        + [jax.ShapeDtypeStruct((256, 160), F32)] * 3,
        in_specs=[away] * 11 + [whole],
        out_specs=[away] + [whole] * 3,
        scratch_shapes=[
            pltpu.VMEM((256, 4096), BF),
            pltpu.VMEM((256, 4096), BF),
            pltpu.VMEM((3, 4096, 160), BF),
            pltpu.VMEM((4096, 256), BF),
            pltpu.SemaphoreType.DMA((7,)),
            pltpu.SemaphoreType.DMA((20,)),
        ],
        compiler_params=params(),
        cost_estimate=pl.CostEstimate(flops=COST, bytes_accessed=10**6, transcendentals=0),
        name="base",
    )(*left, *right, gate_base, up_base, out_base, unit)


def layer_kernel(
    place,
    own_far,
    other_far,
    l0,
    l1,
    l2,
    l3,
    r0,
    r1,
    r2,
    r3,
    x_rows_far,
    pair,
    pair_t,
    scales,
    window,
    gate_part,
    up_part,
    grad_part,
    keep_far,
    send_far,
    own,
    other,
    x_cols,
    x_rows,
    dy,
    near,
    tall,
    e0,
    w1,
    keep,
    send,
    sems,
    piece_sems,
):
    mine = place[1]
    count = [0]
    waits = {}

    def bring(key, source, target):
        copy = pltpu.make_async_copy(source, target, sems.at[count[0]])
        count[0] += 1
        copy.start()
        waits[key] = copy

    for m in range(2):
        bring(("own", m), own_far.at[m], own.at[m])
        bring(("other", m), other_far.at[m], other.at[m])
    first, late = collect((l0, l1, l2, l3), (r0, r1, r2, r3), x_cols, dy, piece_sems)
    bring("x_rows", x_rows_far, x_rows)

    factors = ((D**-0.5) * (128**-0.5), (FF**-0.5) * (128**-0.5))
    tiles = [slice(128 * kt, 128 * (kt + 1)) for kt in range(5)]
    grid, grid_t = pair[mine], pair_t[mine]

    def widen(m, put):
        waits[("own", m)].wait()
        waits[("other", m)].wait()
        for kt in range(5):
            near[0, kt] = own[m, :, tiles[kt]].astype(F32)
            near[1, kt] = other[m, :, tiles[kt]].astype(F32)
        for b in range(8):
            block = jnp.concatenate(
                [
                    jnp.concatenate(
                        [near[side, kt, pl.ds(b, 64, stride=8), :] for kt in range(5)], axis=1
                    )
                    for side in range(2)
                ],
                axis=0,
            ).astype(BF)
            put(b, dot(grid, block) * (scales[m, b : b + 1, :] * factors[m]))

    def put0(b, wide):
        e0[128 * b : 128 * (b + 1), :] = wide.astype(BF)

    def put1(b, wide):
        for kt in range(5):
            tall[kt, 128 * b : 128 * (b + 1), :] = wide[:, tiles[kt]]

    widen(0, put0)
    for copy in first + late + [waits["x_rows"]]:
        copy.wait()
    widen(1, put1)
    for w in range(32):
        for kt in range(5):
            v, jt = divmod(5 * w + kt, 32)
            w1[32 * v : 32 * (v + 1), 128 * jt : 128 * (jt + 1)] = tall[
                kt, pl.ds(w, 32, stride=32), :
            ].astype(BF)
    gate = gate_part[...]
    for q in range(4):
        part = dot(x_cols[:, 1024 * q : 1024 * (q + 1)], e0[:, 128 * q : 128 * q + 256])
        high = part.astype(BF)
        low = (part - high.astype(F32)).astype(BF)
        gate = gate + dot(high, window[q]) + dot(low, window[q])
    up = up_part[...]
    grad = grad_part[...] + dot_t(dy[...], w1[...])
    argument = 0.7978845608028654 * (gate + 0.044715 * gate * gate * gate)
    tangent = jnp.tanh(argument)
    half = 0.5 * (1.0 + tangent)
    hidden = (gate * half * up).astype(BF)
    slope = half + 0.5 * gate * (1.0 - tangent * tangent) * 0.7978845608028654 * (
        1.0 + 0.134145 * gate * gate
    )
    gate_grad = (grad * up * slope).astype(BF)
    out_grad = dot_l(hidden, dy[...])
    for w in range(32):
        for kt in range(5):
            v, jt = divmod(5 * w + kt, 32)
            tall[kt, pl.ds(w, 32, stride=32), :] = out_grad[
                32 * v : 32 * (v + 1), 128 * jt : 128 * (jt + 1)
            ]

    def leave(m, get):
        for b in range(8):
            back = dot(grid_t, (get(b) * (scales[m, b : b + 1, :] * factors[m])).astype(BF))
            for kt in range(5):
                near[0, kt, pl.ds(b, 64, stride=8), :] = back[0:64, tiles[kt]]
                near[1, kt, pl.ds(b, 64, stride=8), :] = back[64:128, tiles[kt]]
        for kt in range(5):
            send[m, :, tiles[kt]] = near[1, kt].astype(BF)
            keep[m, :, tiles[kt]] = near[0, kt].astype(BF)
        bring(("send", m), send.at[m], send_far.at[m])
        bring(("keep", m), keep.at[m], keep_far.at[m])

    def rows_of(b):
        return jnp.concatenate([tall[kt, 128 * b : 128 * (b + 1), :] for kt in range(5)], axis=1)

    leave(1, rows_of)
    windows = [dot_t(gate_grad, window[q]).astype(BF) for q in range(4)]

    for q in range(4):
        part = dot(x_rows[1024 * q : 1024 * (q + 1), :], windows[q])
        tall[q] = part[:, 0:128] + tall[q] if q else part[:, 0:128]
        tall[q + 1] = part[:, 128:256]

    leave(0, rows_of)
    for m in range(2):
        for side in ("send", "keep"):
            waits[(side, m)].wait()


def layer_call(place, own, other, left, right, x_rows, *args):
    whole = pl.BlockSpec(memory_space=pltpu.VMEM)
    away = pl.BlockSpec(memory_space=pl.ANY)
    return pl.pallas_call(
        layer_kernel,
        out_shape=[jax.ShapeDtypeStruct((2, 512, 640), BF)] * 2,
        in_specs=[pl.BlockSpec(memory_space=pltpu.SMEM)] + [away] * 11 + [whole] * len(args),
        out_specs=[away] * 2,
        scratch_shapes=[
            pltpu.VMEM((2, 512, 640), BF),
            pltpu.VMEM((2, 512, 640), BF),
            pltpu.VMEM((256, 4096), BF),
            pltpu.VMEM((4096, 256), BF),
            pltpu.VMEM((256, 4096), BF),
            pltpu.VMEM((2, 5, 512, 128), F32),
            pltpu.VMEM((5, 1024, 128), F32),
            pltpu.VMEM((1024, 640), BF),
            pltpu.VMEM((160, 4096), BF),
            pltpu.VMEM((2, 512, 640), BF),
            pltpu.VMEM((2, 512, 640), BF),
            pltpu.SemaphoreType.DMA((9,)),
            pltpu.SemaphoreType.DMA((20,)),
        ],
        compiler_params=params(),
        name="layer",
    )(place, own, other, *left, *right, x_rows, *args)


def shifted(item, axis):
    return [item] + [
        lax.ppermute(item, axis, [(i, (i + by) % 4) for i in range(4)]) for by in (1, 2, 3)
    ]


def hop(item, axis, by):
    pairs = [
        (4 * core + i, 4 * core + (i + (by if core == 0 else -by)) % 4)
        for core in range(2)
        for i in range(4)
    ]
    return lax.ppermute(item, ("co", axis), pairs)


def near_two(item, axis):
    return [hop(item, axis, by) for by in (1, 3)]


def across(back, axis):
    return hop(back, axis, 1)


def swap_core(item):
    return lax.ppermute(item, "co", [(0, 1), (1, 0)])


def mixers(order):
    block = jnp.arange(512, dtype=jnp.int32)

    def build(left, right):
        both = (left >> 3) & (right >> 3)
        both = both ^ (both >> 4)
        both = both ^ (both >> 2)
        both = both ^ (both >> 1)
        sign = 1 - 2 * (both & 1)
        return jnp.where((left & 7) == (right & 7), sign, 0).astype(BF)

    return build(order[:, None], block[None, :]), build(block[:, None], order[None, :])


def on_device(
    tokens,
    cotangent,
    gate_base,
    up_base,
    out_base,
    subspace,
    sign_flips,
    fast_gains,
    fast_scales,
    block_orders,
):
    const = tables()
    which, core = lax.axis_index("zh"), lax.axis_index("co")
    place = jnp.stack([which, core]).astype(jnp.int32)
    signs = sign_flips.reshape(2, 1024, 640)

    both, place = lax.optimization_barrier((jnp.concatenate([tokens, cotangent], axis=0), place))
    slots = shifted(both, "zl")
    first = lift_call(place, subspace, signs, const["half"])
    left, right = part_call(slots, const["apart"], const["columns"])
    first, left, right = lax.optimization_barrier((first, left, right))
    left_near, right_near = near_two(left, "x"), near_two(right, "y")
    block_orders, fast_gains, *left_near = lax.optimization_barrier(
        (block_orders, fast_gains, *left_near)
    )
    order = lax.dynamic_index_in_dim(block_orders, which, 0, keepdims=False)
    forward, adjoint = mixers(order)
    gains = lax.dynamic_slice(fast_gains, (which, 0, core, 0), (1, 512, 1, 640)).reshape(512, 640)
    left_far, right_far = across(left_near[0], "x"), across(right_near[0], "y")
    left_far, right_far, forward, adjoint, gains = lax.optimization_barrier(
        (left_far, right_far, forward, adjoint, gains)
    )
    left, right = join_call(
        [left, left_near[0], left_far, left_near[1]],
        [right, right_near[0], right_far, right_near[1]],
    )
    stage = (left, right)
    left_near, right_near = near_two(left, "y"), near_two(right, "x")
    first = lax.all_to_all(first.reshape(64, 8, 640), FSDP, split_axis=0, concat_axis=0, tiled=True)

    h512 = const["h512"]
    second = middle_call(forward, gains, h512, first.reshape(512, 640), stage)
    _, left_near, right_near, bases = lax.optimization_barrier(
        (second, left_near, right_near, (gate_base.T, up_base.T, out_base))
    )
    second = lax.all_to_all(
        second.reshape(128, 8, 640), HALVES, split_axis=0, concat_axis=0, tiled=True
    ).reshape(2, 512, 640)
    left = [left, left_near[0], across(left_near[0], "y"), left_near[1]]
    right = [right, right_near[0], across(right_near[0], "x"), right_near[1]]
    sorted_bases = sort_call(*bases, const["order"], const["columns"])
    prepared = base_call(left, right, *sorted_bases, const["unit"])
    second, *prepared = lax.optimization_barrier((second, *prepared))
    other = swap_core(second)
    keep, send = layer_call(
        place,
        second,
        other,
        left,
        right,
        prepared[0],
        const["pair"],
        const["pair_t"],
        fast_scales,
        const["window"],
        *prepared[1:],
    )
    backs = (keep.astype(F32) + swap_core(send).astype(F32)).astype(BF)
    backs = lax.all_to_all(
        backs.reshape(128, 8, 640), HALVES, split_axis=0, concat_axis=0, tiled=True
    ).reshape(2, 512, 640)
    folded = revert_call(adjoint, gains, h512, backs)
    folded = lax.all_to_all(
        folded.reshape(64, 8, 640), FSDP, split_axis=0, concat_axis=0, tiled=True
    )
    part = land_call(place, signs, const["half_t"], folded.reshape(512, 640))
    part = part + swap_core(part)
    return part + lax.ppermute(part, "zh", [(0, 1), (1, 0)])


def solution(mesh):
    split = Mesh(mesh.devices.reshape(2, 2, 4, 4, 4), AXES)
    group = ("zh", "co")
    in_specs = (
        P(group + FSDP, None),
        P(group + FSDP, None),
        P(None, FSDP),
        P(None, FSDP),
        P(FSDP, None),
        P(FSDP, None),
        P(None, FSDP, None, None),
        P(None, None, FSDP, None),
        P(None, FSDP, None),
        P(),
    )
    return jax.shard_map(
        on_device, mesh=split, in_specs=in_specs, out_specs=P(FSDP, None), check_vma=False
    )
```
